32 devices in a mesh: region: 4 (over z), gx: 4 (over y, x), gy: 2 (over core).
Axes of the slice: x: 2, y: 2, z: 4, core: 2. Of those that a mesh axis runs over, the one named last changes fastest.
Arguments:
- spins: float32 [3, 8, 128, 256], P(None, 'region', 'gx', 'gy'), may hold values from -1 to 1, as said below
- uniforms: float32 [2, 8, 128, 256], P(None, 'region', 'gx', 'gy'), may hold values from 0 to 1
- trials: float32 [2, 3, 8, 128, 256], P(None, None, 'region', 'gx', 'gy'), may hold values from -1 to 1
- exch_kernel: float32 [3, 3, 3], replicated, may hold values from -0.5 to 1
- film_m: float32 [3, 2048, 512], P(None, ('region', 'gx'), 'gy'), may hold values from -1 to 1, as said below
- film_anis: float32 [2048, 512], P(('region', 'gx'), 'gy'), may hold values from 0.2 to 2
Outputs:
- spins_out: float32 [3, 8, 128, 256], P(None, 'region', 'gx', 'gy')
- film_out: float32 [3, 2048, 512], P(None, ('region', 'gx'), 'gy')
The draws below stay inside these ranges and needn't reach their ends.
Inputs may be any that keep to these rules, and one draw needn't show every extreme that they name: `spins`: the three components of each site form a unit vector. `film_m`: the three components of each cell form a unit vector.
All inputs are finite; a program needn't handle non-finite values.
Results may differ from the reference program's by a relative error of at most 0.0001.
Values sent between devices are 32-bit elements; how exact they have to be, the bound alone decides.
A program may use at most 64 MiB of HBM per device.

```python
import math
import jax
import jax.numpy as jnp
from jax import lax

K = 8
SWEEPS = 2
AL = 8
AX = 128
AY = 256
FX = 2048
FY = 512


def unit_field(key, shape):
    first_key, second_key = jax.random.split(key)
    height = jax.random.uniform(first_key, shape, jnp.float32, -1.0, 1.0)
    azimuth = jax.random.uniform(second_key, shape, jnp.float32, -math.pi, math.pi)
    radius = jnp.sqrt(jnp.maximum(1.0 - height * height, 0.0))
    return jnp.stack([radius * jnp.cos(azimuth), radius * jnp.sin(azimuth), height])


def draw_spins(key, part):
    return unit_field(jax.random.fold_in(key, 11), (AL, AX, AY))


def draw_film_m(key, part):
    return unit_field(jax.random.fold_in(key, 23), (FX, FY))


def level_of(stream_key, extent, shards, least, largest):
    loudness, own = 1.0, jax.random.fold_in(stream_key, 6)
    for axis_at, parts in shards:
        draws = jnp.exp(jax.random.uniform(jax.random.fold_in(own, axis_at), (parts,), jnp.float32, least / len(shards), largest / len(shards)))
        loudness = loudness * jnp.repeat(draws, extent[axis_at] // parts).reshape([-1 if axis == axis_at else 1 for axis in range(len(extent))])
    return loudness


def setup_inputs(seed: int = 0) -> dict:
    keys = jax.random.split(jax.random.key(seed), 7)
    spins = draw_spins(jax.random.fold_in(keys[6], 71), 0)
    uniforms = jnp.clip(1.0 * jax.random.uniform(keys[1], (SWEEPS, AL, AX, AY), jnp.float32) ** level_of(keys[1], (SWEEPS, AL, AX, AY), ((1, 4), (2, 4), (3, 2)), -0.2, 0.2), 0.0, 1.0)
    trials = jnp.clip(jax.random.uniform(keys[2], (SWEEPS, 3, AL, AX, AY), jnp.float32, -1.0, 1.0) * level_of(keys[2], (SWEEPS, 3, AL, AX, AY), ((2, 4), (3, 4), (4, 2)), -0.4, 0.0), -1.0, 1.0)
    exch_kernel = jnp.clip(jax.random.uniform(keys[3], (3, 3, 3), jnp.float32, -0.5, 1.0), -0.5, 1.0)
    film_m = draw_film_m(jax.random.fold_in(keys[6], 71), 0)
    film_anis = jnp.clip(jnp.exp(math.log(2.0) - 2.3025851 * jax.random.uniform(keys[5], (FX, FY), jnp.float32) ** level_of(keys[5], (FX, FY), ((0, 16), (1, 2)), -0.2, 0.2)), 0.2, 2.0)
    return {"spins": spins, "uniforms": uniforms, "trials": trials, "exch_kernel": exch_kernel, "film_m": film_m, "film_anis": film_anis}


coupling_down = 1.0
anisotropy = 0.5
inverse_temp = 2.0
softness = 0.05
step_cone = 0.4
coupling_up = 2.0
damping = 0.1
time_step = 0.05

def normalized(vector):
    return vector / jnp.sqrt(lax.optimization_barrier(jnp.sum(vector * vector, axis=0, keepdims=True)))

def apply_kernel(matrix, vector):
    return jnp.stack([matrix[component, 0] * vector[0] + matrix[component, 1] * vector[1] + matrix[component, 2] * vector[2] for component in range(3)])

def apply_transposed(matrix, vector):
    return jnp.stack([matrix[0, component] * vector[0] + matrix[1, component] * vector[1] + matrix[2, component] * vector[2] for component in range(3)])

def local_field(padded, exch_kernel):
    forward = (padded[:, 2:, 1:-1, 1:-1], padded[:, 1:-1, 2:, 1:-1], padded[:, 1:-1, 1:-1, 2:])
    backward = (padded[:, :-2, 1:-1, 1:-1], padded[:, 1:-1, :-2, 1:-1], padded[:, 1:-1, 1:-1, :-2])
    summed = apply_kernel(exch_kernel[0], forward[0]) + apply_transposed(exch_kernel[0], backward[0])
    for direction in (1, 2):
        summed = summed + apply_kernel(exch_kernel[direction], forward[direction])
        summed = summed + apply_transposed(exch_kernel[direction], backward[direction])
    return summed

def metropolis(spins, padded, exch_kernel, film_near, trial_move, uniform_draw, colour_mask):
    field_sum = local_field(padded, exch_kernel) + coupling_down * film_near
    proposal = normalized(spins + step_cone * trial_move)
    change = -lax.optimization_barrier(jnp.sum((proposal - spins) * field_sum, axis=0)) - anisotropy * (proposal[2] * proposal[2] - spins[2] * spins[2])
    accept = jnp.exp(jnp.minimum(-inverse_temp * change, 0.0))
    weight = jax.nn.sigmoid((accept - uniform_draw) / softness)
    blended = normalized((1.0 - weight) * spins + weight * proposal)
    return jnp.where(colour_mask[None], blended, spins)

def cross_product(left, right):
    return jnp.stack([left[1] * right[2] - left[2] * right[1], left[2] * right[0] - left[0] * right[2], left[0] * right[1] - left[1] * right[0]])

def film_rate(magnet, padded, film_anis, interface):
    laplace_sum = padded[:, 2:, 1:-1] + padded[:, :-2, 1:-1] + padded[:, 1:-1, 2:] + padded[:, 1:-1, :-2] - 4.0 * magnet
    field_sum = laplace_sum + coupling_up * interface
    field_sum = jnp.stack([field_sum[0], field_sum[1], field_sum[2] + film_anis * magnet[2]])
    precession = cross_product(magnet, field_sum)
    relaxation = cross_product(magnet, precession)
    return -(precession + damping * relaxation) / (1.0 + damping * damping)

def reference(spins, uniforms, trials, exch_kernel, film_m, film_anis):
    cells_x = AX // K
    cells_y = AY // K
    film_block = film_m[:, :cells_x, :cells_y]
    film_cells = jnp.repeat(jnp.repeat(film_block, K, axis=1), K, axis=2)
    layer_pos = jnp.arange(AL, dtype=jnp.int32)
    film_near = jnp.broadcast_to(film_cells[:, None], (3, AL, AX, AY))
    parity = (layer_pos[:, None, None] + jnp.arange(AX, dtype=jnp.int32)[None, :, None] + jnp.arange(AY, dtype=jnp.int32)[None, None, :]) % 2
    for sweep_index in range(SWEEPS):
        for colour in (0, 1):
            padded = jnp.pad(spins, ((0, 0), (1, 1), (1, 1), (1, 1)))
            spins = metropolis(spins, padded, exch_kernel, film_near, trials[sweep_index], uniforms[sweep_index], parity == colour)
    averages = spins[:, 0].reshape(3, cells_x, K, cells_y, K).mean(axis=(2, 4))
    interface = jnp.pad(averages, ((0, 0), (0, FX - cells_x), (0, FY - cells_y)))
    rate_start = film_rate(film_m, jnp.pad(film_m, ((0, 0), (1, 1), (1, 1))), film_anis, interface)
    predicted = film_m + time_step * rate_start
    rate_trial = film_rate(predicted, jnp.pad(predicted, ((0, 0), (1, 1), (1, 1))), film_anis, interface)
    corrected = film_m + 0.5 * time_step * (rate_start + rate_trial)
    return (spins, normalized(corrected))
```

```python
import functools

import jax
import jax.numpy as jnp
from jax import lax
from jax.experimental import pallas as pl
from jax.experimental.pallas import tpu as pltpu
from jax.sharding import PartitionSpec as P

K = 8
SWEEPS = 2


coupling_down = 1.0
anisotropy = 0.5
inverse_temp = 2.0
softness = 0.05
step_cone = 0.4
coupling_up = 2.0
damping = 0.1
time_step = 0.05


def extended(cells, sides, width):
    for axis, dim in sides:
        count = lax.axis_size(axis)
        ends = count - 1
        head = lax.slice_in_dim(cells, 0, width, axis=dim)
        tail = lax.slice_in_dim(cells, cells.shape[dim] - width, cells.shape[dim], axis=dim)
        cells = jnp.concatenate(
            [
                lax.ppermute(tail, axis, [(i, (i + 1) % count) for i in range(ends)]),
                cells,
                lax.ppermute(head, axis, [((i + 1) % count, i) for i in range(ends)]),
            ],
            axis=dim,
        )
    return cells


def spread(value, axis, source):
    kept = jnp.where(lax.axis_index(axis) == source, value, 0).astype(value.dtype)
    return lax.psum(kept, axis)


def normalized(vector):
    return vector / jnp.sqrt(jnp.sum(vector * vector, axis=0, keepdims=True))


def apply_kernel(matrix, vector):
    return jnp.stack(
        [
            matrix[component, 0] * vector[0]
            + matrix[component, 1] * vector[1]
            + matrix[component, 2] * vector[2]
            for component in range(3)
        ]
    )


def apply_transposed(matrix, vector):
    return jnp.stack(
        [
            matrix[0, component] * vector[0]
            + matrix[1, component] * vector[1]
            + matrix[2, component] * vector[2]
            for component in range(3)
        ]
    )


def local_field(padded, exch_kernel):
    forward = (padded[:, 2:, 1:-1, 1:-1], padded[:, 1:-1, 2:, 1:-1], padded[:, 1:-1, 1:-1, 2:])
    backward = (padded[:, :-2, 1:-1, 1:-1], padded[:, 1:-1, :-2, 1:-1], padded[:, 1:-1, 1:-1, :-2])
    summed = apply_kernel(exch_kernel[0], forward[0]) + apply_transposed(
        exch_kernel[0], backward[0]
    )
    for direction in (1, 2):
        summed = summed + apply_kernel(exch_kernel[direction], forward[direction])
        summed = summed + apply_transposed(exch_kernel[direction], backward[direction])
    return summed


def metropolis(spins, padded, exch_kernel, film_near, trial_move, uniform_draw, colour_mask):
    field_sum = local_field(padded, exch_kernel) + coupling_down * film_near
    proposal = normalized(spins + step_cone * trial_move)
    change = -jnp.sum((proposal - spins) * field_sum, axis=0) - anisotropy * (
        proposal[2] * proposal[2] - spins[2] * spins[2]
    )
    accept = jnp.exp(jnp.minimum(-inverse_temp * change, 0.0))
    weight = jax.nn.sigmoid((accept - uniform_draw) / softness)
    blended = normalized((1.0 - weight) * spins + weight * proposal)
    return jnp.where(colour_mask[None], blended, spins)


def cross_product(left, right):
    return jnp.stack(
        [
            left[1] * right[2] - left[2] * right[1],
            left[2] * right[0] - left[0] * right[2],
            left[0] * right[1] - left[1] * right[0],
        ]
    )


def film_rate(magnet, padded, film_anis, interface):
    laplace_sum = (
        padded[:, 2:, 1:-1]
        + padded[:, :-2, 1:-1]
        + padded[:, 1:-1, 2:]
        + padded[:, 1:-1, :-2]
        - 4.0 * magnet
    )
    field_sum = laplace_sum + coupling_up * interface
    field_sum = jnp.stack([field_sum[0], field_sum[1], field_sum[2] + film_anis * magnet[2]])
    precession = cross_product(magnet, field_sum)
    relaxation = cross_product(magnet, precession)
    return -(precession + damping * relaxation) / (1.0 + damping * damping)


def film_halo(magnet):
    return extended(magnet, ((("region", "gx"), 1), ("gy", 2)), 1)


def body_general(spins, uniforms, trials, exch_kernel, film_m, film_anis):
    layers_dev = spins.shape[1]
    rows_x = spins.shape[2]
    rows_y = spins.shape[3]
    piece_x = rows_x // K
    piece_y = rows_y // K
    gx_count = lax.axis_size("gx")
    gy_count = lax.axis_size("gy")
    region_pos = lax.axis_index("region")
    gx_pos = lax.axis_index("gx")
    gy_pos = lax.axis_index("gy")
    first_tile = (region_pos == 0) & (gx_pos == 0) & (gy_pos == 0)
    film_block = film_m[:, : piece_x * gx_count, : piece_y * gy_count]
    stack_spins, unif_all, trial_all = (spins, uniforms, trials)
    layer_pos = region_pos * layers_dev + jnp.arange(layers_dev, dtype=jnp.int32)
    film_block = spread(film_block, ("region", "gx", "gy"), 0)
    own_cells = lax.dynamic_slice(
        film_block, (jnp.int32(0), gx_pos * piece_x, gy_pos * piece_y), (3, piece_x, piece_y)
    )
    film_cells = jnp.repeat(jnp.repeat(own_cells, K, axis=1), K, axis=2)
    film_near = jnp.broadcast_to(film_cells[:, None], (3, stack_spins.shape[1], rows_x, rows_y))
    x_global = gx_pos * rows_x + jnp.arange(rows_x, dtype=jnp.int32)
    y_global = gy_pos * rows_y + jnp.arange(rows_y, dtype=jnp.int32)
    parity = (layer_pos[:, None, None] + x_global[None, :, None] + y_global[None, None, :]) % 2
    for sweep_index in range(SWEEPS):
        for colour in (0, 1):
            padded = extended(stack_spins, (("region", 1), ("gx", 2), ("gy", 3)), 1)
            stack_spins = metropolis(
                stack_spins,
                padded,
                exch_kernel,
                film_near,
                trial_all[sweep_index],
                unif_all[sweep_index],
                parity == colour,
            )
    averages = stack_spins[:, 0].reshape(3, piece_x, K, piece_y, K).mean(axis=(2, 4))
    gathered = lax.all_gather(averages[None], ("gx", "gy"), axis=0, tiled=True)
    assembled = (
        gathered.reshape(gx_count, gy_count, 3, piece_x, piece_y)
        .transpose(2, 0, 3, 1, 4)
        .reshape(3, gx_count * piece_x, gy_count * piece_y)
    )
    padded_block = jnp.pad(
        assembled,
        (
            (0, 0),
            (0, film_m.shape[1] - assembled.shape[1]),
            (0, film_m.shape[2] - assembled.shape[2]),
        ),
    )
    interface = jnp.where(first_tile, padded_block, 0.0)
    rate_start = film_rate(film_m, film_halo(film_m), film_anis, interface)
    predicted = film_m + time_step * rate_start
    rate_trial = film_rate(predicted, film_halo(predicted), film_anis, interface)
    corrected = film_m + 0.5 * time_step * (rate_start + rate_trial)
    return (stack_spins, normalized(corrected))


LANES = 128
EDGE = 8
ROUNDS = 2 * SWEEPS
MESH = pl.DeviceIdType.MESH


def kernel_fits(spins, film_m, counts):
    _, gx_count, gy_count = counts
    _, _, rows_x, rows_y = spins.shape
    cells_x, cells_y = rows_x // K * gx_count, rows_y // K * gy_count
    return (
        rows_y == LANES
        and rows_x % 16 == 0
        and EDGE % (rows_x // K) == 0
        and cells_x % EDGE == 0
        and 3 * cells_y <= LANES
        and 3 * (rows_x // K) <= 16
        and film_m.shape[1] % 16 == 0
        and cells_x + 16 <= film_m.shape[1]
        and film_m.shape[2] % LANES == 0
        and cells_y + 2 <= film_m.shape[2]
        and 3 * spins.shape[1] <= EDGE
    )


def unit(vector):
    scale = lax.rsqrt(vector[0] * vector[0] + vector[1] * vector[1] + vector[2] * vector[2])
    return [part * scale for part in vector]


def cross(left, right):
    return [
        left[1] * right[2] - left[2] * right[1],
        left[2] * right[0] - left[0] * right[2],
        left[0] * right[1] - left[1] * right[0],
    ]


def fused_kernel(
    counts,
    exch,
    spins_hbm,
    unif_hbm,
    trial_hbm,
    film_hbm,
    anis_hbm,
    spins_out,
    film_out,
    stack,
    unif,
    trial,
    film_near,
    film,
    trial_film,
    half_film,
    anis,
    x_send,
    x_recv,
    y_send,
    y_recv,
    z_recv,
    fx_send,
    fx_recv,
    fy_send,
    fy_recv,
    cell_all,
    cell_own,
    mean_send,
    mean_recv,
    inter,
    local_sem,
    send_sem,
    recv_sem,
    film_send_sem,
    film_recv_sem,
    cell_send_sem,
    cell_recv_sem,
    mean_send_sem,
    mean_recv_sem,
):
    regions, gx_count, gy_count = counts
    layers, rows = spins_hbm.shape[1], spins_hbm.shape[2]
    film_rows, film_cols = film_hbm.shape[1], film_hbm.shape[2]
    piece_x, piece_y = rows // K, LANES // K
    cells_x, cells_y = piece_x * gx_count, piece_y * gy_count
    per_tile = EDGE // piece_x
    inner = pl.ds(EDGE, rows)
    film_inner = pl.ds(EDGE, film_rows)
    region = lax.axis_index("region")
    gx = lax.axis_index("gx")
    gy = lax.axis_index("gy")
    first = (region == 0) & (gx == 0) & (gy == 0)
    not_first = jnp.logical_not(first)

    places = [
        (region > 0, (region - 1, gx, gy)),
        (region < regions - 1, (region + 1, gx, gy)),
        (gx > 0, (region, gx - 1, gy)),
        (gx < gx_count - 1, (region, gx + 1, gy)),
        (gy > 0, (region, gx, gy - 1)),
        (gy < gy_count - 1, (region, gx, gy + 1)),
    ]
    line = region * gx_count + gx
    film_places = [
        (line > 0, ((line + gx_count * regions - 1) // gx_count % regions, (gx + gx_count - 1) % gx_count, gy)),
        (line < regions * gx_count - 1, ((line + 1) // gx_count % regions, (gx + 1) % gx_count, gy)),
        places[4],
        places[5],
    ]

    loads = [
        pltpu.make_async_copy(source, target, local_sem.at[at])
        for at, (source, target) in enumerate(
            [
                (spins_hbm, stack.at[0, :, :, inner, :]),
                (film_hbm, film.at[:, film_inner, :]),
                (trial_hbm, trial),
                (unif_hbm, unif),
                (anis_hbm, anis),
            ]
        )
    ]
    for load in loads:
        load.start()

    barrier = pltpu.get_barrier_semaphore()
    for there, place in places + film_places[:2]:

        @pl.when(there)
        def _(place=place):
            pl.semaphore_signal(barrier, inc=1, device_id=place, device_id_type=MESH)

    @pl.when(not_first)
    def _():
        pl.semaphore_signal(barrier, inc=1, device_id=(0, 0, 0), device_id_type=MESH)

    @pl.when(first)
    def _():
        for gx_at in range(gx_count):
            for gy_at in range(gy_count):
                if gx_at or gy_at:
                    pl.semaphore_signal(barrier, inc=1, device_id=(0, gx_at, gy_at), device_id_type=MESH)

    lane = lax.broadcasted_iota(jnp.int32, (rows, LANES), 1)
    film_lane = lax.broadcasted_iota(jnp.int32, (film_rows, LANES), 1)

    def halo(turn, way):
        if way < 2:
            source = stack.at[turn, :, 0 if way == 0 else layers - 1, inner, :]
            return source, z_recv
        if way < 4:
            return x_send.at[turn, way - 2], x_recv
        return y_send.at[turn, way - 4], y_recv

    def halo_copy(turn, way, slot):
        source, target = halo(turn, way)
        return pltpu.make_async_remote_copy(
            src_ref=source,
            dst_ref=target.at[turn, slot % 2],
            send_sem=send_sem.at[turn, way],
            recv_sem=recv_sem.at[turn, slot],
            device_id=places[way][1],
            device_id_type=MESH,
        )

    def film_copy(turn, way, slot):
        source, target = (fx_send, fx_recv) if way < 2 else (fy_send, fy_recv)
        return pltpu.make_async_remote_copy(
            src_ref=source.at[turn, way % 2],
            dst_ref=target.at[turn, slot % 2],
            send_sem=film_send_sem.at[turn, way],
            recv_sem=film_recv_sem.at[turn, slot],
            device_id=film_places[way][1],
            device_id_type=MESH,
        )

    def pack_halo(turn):
        right = jnp.zeros((rows, LANES), jnp.float32)
        left = right
        for part in range(3):
            for layer in range(layers):
                at = part * layers + layer
                block = stack[turn, part, layer, inner, :]
                x_send[turn, 0, at : at + 1, :] = stack[turn, part, layer, EDGE : EDGE + 1, :]
                x_send[turn, 1, at : at + 1, :] = stack[turn, part, layer, EDGE + rows - 1 : EDGE + rows, :]
                left = jnp.where(lane == at, pltpu.roll(block, at, 1) if at else block, left)
                right = jnp.where(lane == at, pltpu.roll(block, at + 1, 1), right)
        y_send[turn, 0] = left
        y_send[turn, 1] = right

    def send_halo(turn, ways):
        for way in ways:

            @pl.when(places[way][0])
            def _(way=way):
                halo_copy(turn, way, way ^ 1).start()

    def take_halo(turn):
        for way in range(6):

            @pl.when(places[way][0])
            def _(way=way):
                halo_copy(turn, way, way).wait_recv()

        for part in range(3):
            for layer in range(layers):
                at = part * layers + layer
                stack[turn, part, layer, EDGE - 1 : EDGE, :] = x_recv[turn, 0, at : at + 1, :]
                stack[turn, part, layer, EDGE + rows : EDGE + rows + 1, :] = x_recv[turn, 1, at : at + 1, :]

    def pack_film(turn, source):
        left = jnp.zeros((film_rows, LANES), jnp.float32)
        right = left
        for part in range(3):
            fx_send[turn, 0, part : part + 1, :] = source[part, EDGE : EDGE + 1, :]
            fx_send[turn, 1, part : part + 1, :] = source[part, EDGE + film_rows - 1 : EDGE + film_rows, :]
            head = source[part, film_inner, :LANES]
            tail = source[part, film_inner, film_cols - LANES :]
            left = jnp.where(film_lane == part, pltpu.roll(head, part, 1) if part else head, left)
            right = jnp.where(film_lane == part, pltpu.roll(tail, part + 1, 1), right)
        fy_send[turn, 0] = left
        fy_send[turn, 1] = right

    def send_film(turn):
        for way in range(4):

            @pl.when(film_places[way][0])
            def _(way=way):
                film_copy(turn, way, way ^ 1).start()

    def take_film(turn, target):
        for way in range(4):

            @pl.when(film_places[way][0])
            def _(way=way):
                film_copy(turn, way, way).wait_recv()

        for part in range(3):
            target[part, EDGE - 1 : EDGE, :] = fx_recv[turn, 0, part : part + 1, :]
            target[part, EDGE + film_rows : EDGE + film_rows + 1, :] = fx_recv[turn, 1, part : part + 1, :]

    def rate(turn, source, low, count, with_inter):
        wide = lax.broadcasted_iota(jnp.int32, (count, film_cols), 1)
        repeat = film_cols // LANES
        magnet, field = [], []
        for part in range(3):
            at = EDGE + low
            block = source[part, at : at + count, :]
            before = pltpu.roll(fy_recv[turn, 0, low : low + count, :], (LANES - part) % LANES, 1) if part else fy_recv[turn, 0, low : low + count, :]
            after = pltpu.roll(fy_recv[turn, 1, low : low + count, :], LANES - 1 - part, 1)
            total = source[part, at - 1 : at - 1 + count, :] + source[part, at + 1 : at + 1 + count, :]
            total = total + jnp.where(wide == 0, jnp.concatenate([before] * repeat, 1), pltpu.roll(block, 1, 1))
            total = total + jnp.where(
                wide == film_cols - 1, jnp.concatenate([after] * repeat, 1), pltpu.roll(block, film_cols - 1, 1)
            )
            total = total - 4.0 * block
            if with_inter:
                extra = coupling_up * inter[part, low : low + count, :]
                rest = [jnp.zeros((count, LANES), jnp.float32)] * (repeat - 1)
                total = total + jnp.concatenate([extra] + rest, 1)
            magnet.append(block)
            field.append(total)
        field[2] = field[2] + anis[low : low + count, :] * magnet[2]
        precession = cross(magnet, field)
        relaxation = cross(magnet, precession)
        factor = -1.0 / (1.0 + damping * damping)
        return magnet, [factor * (one + damping * two) for one, two in zip(precession, relaxation)]

    def film_start(low, count, with_inter=False):
        magnet, speed = rate(0, film, low, count, with_inter)
        for part in range(3):
            trial_film[part, EDGE + low : EDGE + low + count, :] = magnet[part] + time_step * speed[part]
            half_film[part, low : low + count, :] = magnet[part] + (0.5 * time_step) * speed[part]

    def film_end(low, count, with_inter=False):
        _, speed = rate(1, trial_film, low, count, with_inter)
        result = unit([half_film[part, low : low + count, :] + (0.5 * time_step) * speed[part] for part in range(3)])
        for part in range(3):
            film_out[part, low : low + count, :] = result[part]

    x_iota = lax.broadcasted_iota(jnp.int32, (rows, LANES), 0)

    def half_sweep(turn):
        sweep, colour = turn // 2, turn % 2
        for layer in range(layers):
            own = [stack[turn, part, layer, inner, :] for part in range(3)]
            proposal = unit([own[part] + step_cone * trial[sweep, part, layer] for part in range(3)])
            around = [[] for _ in range(6)]
            for part in range(3):
                at = part * layers + layer
                around[0].append(z_recv[turn, 0, part] if layer == 0 else stack[turn, part, layer - 1, inner, :])
                around[1].append(z_recv[turn, 1, part] if layer == layers - 1 else stack[turn, part, layer + 1, inner, :])
                around[2].append(stack[turn, part, layer, EDGE - 1 : EDGE - 1 + rows, :])
                around[3].append(stack[turn, part, layer, EDGE + 1 : EDGE + 1 + rows, :])
                before = pltpu.roll(y_recv[turn, 0], LANES - at, 1) if at else y_recv[turn, 0]
                after = pltpu.roll(y_recv[turn, 1], LANES - 1 - at, 1)
                around[4].append(jnp.where(lane == 0, before, pltpu.roll(own[part], 1, 1)))
                around[5].append(jnp.where(lane == LANES - 1, after, pltpu.roll(own[part], LANES - 1, 1)))
            gain = jnp.zeros((rows, LANES), jnp.float32)
            shift = [proposal[part] - own[part] for part in range(3)]
            for part in range(3):
                field = coupling_down * film_near[part]
                for way in range(3):
                    for other in range(3):
                        field = field + exch[9 * way + 3 * part + other] * around[2 * way + 1][other]
                        field = field + exch[9 * way + 3 * other + part] * around[2 * way][other]
                gain = gain + shift[part] * field
            change = -gain - anisotropy * (proposal[2] * proposal[2] - own[2] * own[2])
            accept = jnp.exp(jnp.minimum(-inverse_temp * change, 0.0))
            weight = 1.0 / (1.0 + jnp.exp((unif[sweep, layer] - accept) * (1.0 / softness)))
            blended = unit([own[part] + weight * shift[part] for part in range(3)])
            parity = (region * layers + layer + gx * rows + gy * LANES + x_iota + lane) % 2
            for part in range(3):
                fresh = jnp.where(parity == colour, blended[part], own[part])
                if turn == ROUNDS - 1:
                    spins_out[part, layer] = fresh
                else:
                    stack[turn + 1, part, layer, inner, :] = fresh

    def cell_copy(region_at, gx_at, gy_at):
        number = (region_at * gx_count + gx_at) * gy_count + gy_at
        return pltpu.make_async_remote_copy(
            src_ref=cell_all.at[pl.ds(gx_at // per_tile * EDGE, EDGE), :],
            dst_ref=cell_own,
            send_sem=cell_send_sem.at[number],
            recv_sem=cell_recv_sem,
            device_id=(region_at, gx_at, gy_at),
            device_id_type=MESH,
        )

    others = [
        (region_at, gx_at, gy_at)
        for region_at in reversed(range(regions))
        for gx_at in reversed(range(gx_count))
        for gy_at in reversed(range(gy_count))
        if region_at or gx_at or gy_at
    ]

    def mean_copy(gx_at, gy_at):
        number = gx_at * gy_count + gy_at
        return pltpu.make_async_remote_copy(
            src_ref=mean_send,
            dst_ref=mean_recv.at[number],
            send_sem=mean_send_sem,
            recv_sem=mean_recv_sem.at[number],
            device_id=(0, 0, 0),
            device_id_type=MESH,
        )

    for way in range(6):

        @pl.when(jnp.logical_not(places[way][0]))
        def _(way=way):
            for turn in range(ROUNDS):
                target = halo(turn, way)[1]
                target[turn, way % 2] = jnp.zeros(target.shape[2:], jnp.float32)

    for way in range(4):

        @pl.when(jnp.logical_not(film_places[way][0]))
        def _(way=way):
            target = fx_recv if way < 2 else fy_recv
            for turn in range(2):
                target[turn, way % 2] = jnp.zeros(target.shape[2:], jnp.float32)

    loads[0].wait()
    pack_halo(0)
    loads[1].wait()

    @pl.when(first)
    def _():
        cell_lane = lax.broadcasted_iota(jnp.int32, (cells_x, LANES), 1)
        packed = film[0, EDGE : EDGE + cells_x, :LANES]
        for part in (1, 2):
            moved = pltpu.roll(film[part, EDGE : EDGE + cells_x, :LANES], part * cells_y, 1)
            packed = jnp.where(cell_lane >= part * cells_y, moved, packed)
        cell_all[...] = packed
        cell_own[...] = packed[:EDGE]

    pack_film(0, film)

    expected = sum(there.astype(jnp.int32) for there, _ in places + film_places[:2])
    expected = expected + jnp.where(
        first, regions * gx_count * gy_count - 1, jnp.where(region == 0, 1, 0)
    )
    pl.semaphore_wait(barrier, expected)

    @pl.when(first)
    def _():
        for other in others:
            cell_copy(*other).start()

    send_halo(0, range(6))
    send_film(0)
    for load in loads[2:]:
        load.wait()

    @pl.when(not_first)
    def _():
        cell_copy(0, 0, 0).wait_recv()

    row_at = lax.broadcasted_iota(jnp.int32, (LANES, LANES), 0)
    col_at = lax.broadcasted_iota(jnp.int32, (LANES, LANES), 1)
    pick_row = lax.broadcasted_iota(jnp.int32, (rows, EDGE), 0) // K + gx % per_tile * piece_x
    pick = (lax.broadcasted_iota(jnp.int32, (rows, EDGE), 1) == pick_row).astype(jnp.float32)
    dot = functools.partial(jnp.dot, precision=lax.Precision.HIGHEST, preferred_element_type=jnp.float32)
    cells = jnp.where(
        lax.broadcasted_iota(jnp.int32, (EDGE, LANES), 1) < 3 * cells_y, cell_own[...], 0.0
    )
    tall = dot(pick, cells)
    for part in range(3):
        spread_cols = (row_at == part * cells_y + gy * piece_y + col_at // K).astype(jnp.float32)
        film_near[part] = dot(tall, spread_cols)

    film_steps = list(range(0, film_rows, 16))
    for turn in range(ROUNDS):
        take_halo(turn)
        half_sweep(turn)
        if turn + 1 < ROUNDS:
            pack_halo(turn + 1)
            send_halo(turn + 1, range(6))
        if turn == 0:
            take_film(0, film)
            for low in film_steps:
                film_start(low, 16)
            pack_film(1, trial_film)
            send_film(1)
        if turn == 1:
            take_film(1, trial_film)
            for low in film_steps[: len(film_steps) // 2]:
                film_end(low, 16)
        if turn == 2:
            for low in film_steps[len(film_steps) // 2 :]:
                film_end(low, 16)

    @pl.when(region == 0)
    def _():
        for part in range(3):
            for at in range(piece_x):
                block = spins_out[part, 0, at * K : (at + 1) * K, :]
                mean_send[part * piece_x + at : part * piece_x + at + 1, :] = jnp.sum(block, axis=0, keepdims=True)
        for at in range(3 * piece_x, 16):
            mean_send[at : at + 1, :] = jnp.zeros((1, LANES), jnp.float32)
        gather_cols = jnp.where(col_at == row_at // K + gy * piece_y, 1.0 / (K * K), 0.0)
        mean_send[...] = dot(mean_send[...], gather_cols)

        @pl.when(not_first)
        def _():
            number = gx * gy_count + gy
            pltpu.make_async_remote_copy(
                src_ref=mean_send,
                dst_ref=mean_recv.at[number],
                send_sem=mean_send_sem,
                recv_sem=mean_recv_sem.at[number],
                device_id=(0, 0, 0),
                device_id_type=MESH,
            ).start()

    @pl.when(first)
    def _():
        inter[...] = jnp.zeros(inter.shape, jnp.float32)
        for gx_at in range(gx_count):
            total = jnp.zeros((16, LANES), jnp.float32)
            for gy_at in range(gy_count):
                if gx_at or gy_at:
                    mean_copy(gx_at, gy_at).wait_recv()
                    total = total + mean_recv[gx_at * gy_count + gy_at]
                else:
                    total = total + mean_send[...]
            for part in range(3):
                inter[part, gx_at * piece_x : (gx_at + 1) * piece_x, :] = total[
                    part * piece_x : (part + 1) * piece_x
                ]
        touched = cells_x + EDGE
        for low in range(0, touched, EDGE):
            film_start(low, EDGE, True)
        for low in range(0, touched, EDGE):
            film_end(low, EDGE, True)
        for other in others:
            cell_copy(*other).wait_send()

    @pl.when((region == 0) & not_first)
    def _():
        mean_copy(0, 0).wait_send()

    for turn in range(ROUNDS):
        for way in range(6):

            @pl.when(places[way][0])
            def _(turn=turn, way=way):
                halo_copy(turn, way, way ^ 1).wait_send()

    for turn in range(2):
        for way in range(4):

            @pl.when(film_places[way][0])
            def _(turn=turn, way=way):
                film_copy(turn, way, way ^ 1).wait_send()


def body(spins, uniforms, trials, exch_kernel, film_m, film_anis):
    counts = tuple(lax.axis_size(axis) for axis in ("region", "gx", "gy"))
    if not kernel_fits(spins, film_m, counts):
        return body_general(spins, uniforms, trials, exch_kernel, film_m, film_anis)
    regions, gx_count, gy_count = counts
    _, layers, rows, _ = spins.shape
    _, film_rows, film_cols = film_m.shape
    cells_x = rows // K * gx_count
    tiles = gx_count * gy_count
    dma = pltpu.SemaphoreType.DMA

    def vmem(*shape):
        return pltpu.VMEM(shape, jnp.float32)

    anywhere = pl.BlockSpec(memory_space=pl.ANY)
    inside = pl.BlockSpec(memory_space=pltpu.VMEM)
    return pl.pallas_call(
        functools.partial(fused_kernel, counts),
        out_shape=(
            jax.ShapeDtypeStruct(spins.shape, jnp.float32),
            jax.ShapeDtypeStruct(film_m.shape, jnp.float32),
        ),
        in_specs=[pl.BlockSpec(memory_space=pltpu.SMEM)] + [anywhere] * 5,
        out_specs=(inside, inside),
        scratch_shapes=[
            vmem(ROUNDS, 3, layers, rows + 2 * EDGE, LANES),
            vmem(*uniforms.shape),
            vmem(*trials.shape),
            vmem(3, rows, LANES),
            vmem(3, film_rows + 2 * EDGE, film_cols),
            vmem(3, film_rows + 2 * EDGE, film_cols),
            vmem(3, film_rows, film_cols),
            vmem(film_rows, film_cols),
            vmem(ROUNDS, 2, EDGE, LANES),
            vmem(ROUNDS, 2, EDGE, LANES),
            vmem(ROUNDS, 2, rows, LANES),
            vmem(ROUNDS, 2, rows, LANES),
            vmem(ROUNDS, 2, 3, rows, LANES),
            vmem(2, 2, EDGE, film_cols),
            vmem(2, 2, EDGE, film_cols),
            vmem(2, 2, film_rows, LANES),
            vmem(2, 2, film_rows, LANES),
            vmem(cells_x, LANES),
            vmem(EDGE, LANES),
            vmem(16, LANES),
            vmem(tiles, 16, LANES),
            vmem(3, cells_x + EDGE, LANES),
            dma((5,)),
            dma((ROUNDS, 6)),
            dma((ROUNDS, 6)),
            dma((2, 4)),
            dma((2, 4)),
            dma((regions * tiles,)),
            dma,
            dma,
            dma((tiles,)),
        ],
        compiler_params=pltpu.CompilerParams(
            collective_id=0, has_side_effects=True, vmem_limit_bytes=32 * 1024 * 1024
        ),
    )(exch_kernel.reshape(27), spins, uniforms, trials, film_m, film_anis)


def solution(mesh):
    return jax.shard_map(
        body,
        mesh=mesh,
        in_specs=(
            P(None, "region", "gx", "gy"),
            P(None, "region", "gx", "gy"),
            P(None, None, "region", "gx", "gy"),
            P(),
            P(None, ("region", "gx"), "gy"),
            P(("region", "gx"), "gy"),
        ),
        out_specs=(P(None, "region", "gx", "gy"), P(None, ("region", "gx"), "gy")),
        check_vma=False,
    )
```

```python
import functools

import jax
import jax.numpy as jnp
from jax import lax
from jax.experimental import pallas as pl
from jax.experimental.pallas import tpu as pltpu
from jax.sharding import PartitionSpec as P

K = 8
SWEEPS = 2


coupling_down = 1.0
anisotropy = 0.5
inverse_temp = 2.0
softness = 0.05
step_cone = 0.4
coupling_up = 2.0
damping = 0.1
time_step = 0.05


def extended(cells, sides, width):
    for axis, dim in sides:
        count = lax.axis_size(axis)
        ends = count - 1
        head = lax.slice_in_dim(cells, 0, width, axis=dim)
        tail = lax.slice_in_dim(cells, cells.shape[dim] - width, cells.shape[dim], axis=dim)
        cells = jnp.concatenate(
            [
                lax.ppermute(tail, axis, [(i, (i + 1) % count) for i in range(ends)]),
                cells,
                lax.ppermute(head, axis, [((i + 1) % count, i) for i in range(ends)]),
            ],
            axis=dim,
        )
    return cells


def spread(value, axis, source):
    kept = jnp.where(lax.axis_index(axis) == source, value, 0).astype(value.dtype)
    return lax.psum(kept, axis)


def normalized(vector):
    return vector / jnp.sqrt(jnp.sum(vector * vector, axis=0, keepdims=True))


def apply_kernel(matrix, vector):
    return jnp.stack(
        [
            matrix[component, 0] * vector[0]
            + matrix[component, 1] * vector[1]
            + matrix[component, 2] * vector[2]
            for component in range(3)
        ]
    )


def apply_transposed(matrix, vector):
    return jnp.stack(
        [
            matrix[0, component] * vector[0]
            + matrix[1, component] * vector[1]
            + matrix[2, component] * vector[2]
            for component in range(3)
        ]
    )


def local_field(padded, exch_kernel):
    forward = (padded[:, 2:, 1:-1, 1:-1], padded[:, 1:-1, 2:, 1:-1], padded[:, 1:-1, 1:-1, 2:])
    backward = (padded[:, :-2, 1:-1, 1:-1], padded[:, 1:-1, :-2, 1:-1], padded[:, 1:-1, 1:-1, :-2])
    summed = apply_kernel(exch_kernel[0], forward[0]) + apply_transposed(
        exch_kernel[0], backward[0]
    )
    for direction in (1, 2):
        summed = summed + apply_kernel(exch_kernel[direction], forward[direction])
        summed = summed + apply_transposed(exch_kernel[direction], backward[direction])
    return summed


def metropolis(spins, padded, exch_kernel, film_near, trial_move, uniform_draw, colour_mask):
    field_sum = local_field(padded, exch_kernel) + coupling_down * film_near
    proposal = normalized(spins + step_cone * trial_move)
    change = -jnp.sum((proposal - spins) * field_sum, axis=0) - anisotropy * (
        proposal[2] * proposal[2] - spins[2] * spins[2]
    )
    accept = jnp.exp(jnp.minimum(-inverse_temp * change, 0.0))
    weight = jax.nn.sigmoid((accept - uniform_draw) / softness)
    blended = normalized((1.0 - weight) * spins + weight * proposal)
    return jnp.where(colour_mask[None], blended, spins)


def cross_product(left, right):
    return jnp.stack(
        [
            left[1] * right[2] - left[2] * right[1],
            left[2] * right[0] - left[0] * right[2],
            left[0] * right[1] - left[1] * right[0],
        ]
    )


def film_rate(magnet, padded, film_anis, interface):
    laplace_sum = (
        padded[:, 2:, 1:-1]
        + padded[:, :-2, 1:-1]
        + padded[:, 1:-1, 2:]
        + padded[:, 1:-1, :-2]
        - 4.0 * magnet
    )
    field_sum = laplace_sum + coupling_up * interface
    field_sum = jnp.stack([field_sum[0], field_sum[1], field_sum[2] + film_anis * magnet[2]])
    precession = cross_product(magnet, field_sum)
    relaxation = cross_product(magnet, precession)
    return -(precession + damping * relaxation) / (1.0 + damping * damping)


def film_halo(magnet):
    return extended(magnet, ((("region", "gx"), 1), ("gy", 2)), 1)


def body_general(spins, uniforms, trials, exch_kernel, film_m, film_anis):
    layers_dev = spins.shape[1]
    rows_x = spins.shape[2]
    rows_y = spins.shape[3]
    piece_x = rows_x // K
    piece_y = rows_y // K
    gx_count = lax.axis_size("gx")
    gy_count = lax.axis_size("gy")
    region_pos = lax.axis_index("region")
    gx_pos = lax.axis_index("gx")
    gy_pos = lax.axis_index("gy")
    first_tile = (region_pos == 0) & (gx_pos == 0) & (gy_pos == 0)
    film_block = film_m[:, : piece_x * gx_count, : piece_y * gy_count]
    stack_spins, unif_all, trial_all = (spins, uniforms, trials)
    layer_pos = region_pos * layers_dev + jnp.arange(layers_dev, dtype=jnp.int32)
    film_block = spread(film_block, ("region", "gx", "gy"), 0)
    own_cells = lax.dynamic_slice(
        film_block, (jnp.int32(0), gx_pos * piece_x, gy_pos * piece_y), (3, piece_x, piece_y)
    )
    film_cells = jnp.repeat(jnp.repeat(own_cells, K, axis=1), K, axis=2)
    film_near = jnp.broadcast_to(film_cells[:, None], (3, stack_spins.shape[1], rows_x, rows_y))
    x_global = gx_pos * rows_x + jnp.arange(rows_x, dtype=jnp.int32)
    y_global = gy_pos * rows_y + jnp.arange(rows_y, dtype=jnp.int32)
    parity = (layer_pos[:, None, None] + x_global[None, :, None] + y_global[None, None, :]) % 2
    for sweep_index in range(SWEEPS):
        for colour in (0, 1):
            padded = extended(stack_spins, (("region", 1), ("gx", 2), ("gy", 3)), 1)
            stack_spins = metropolis(
                stack_spins,
                padded,
                exch_kernel,
                film_near,
                trial_all[sweep_index],
                unif_all[sweep_index],
                parity == colour,
            )
    averages = stack_spins[:, 0].reshape(3, piece_x, K, piece_y, K).mean(axis=(2, 4))
    gathered = lax.all_gather(averages[None], ("gx", "gy"), axis=0, tiled=True)
    assembled = (
        gathered.reshape(gx_count, gy_count, 3, piece_x, piece_y)
        .transpose(2, 0, 3, 1, 4)
        .reshape(3, gx_count * piece_x, gy_count * piece_y)
    )
    padded_block = jnp.pad(
        assembled,
        (
            (0, 0),
            (0, film_m.shape[1] - assembled.shape[1]),
            (0, film_m.shape[2] - assembled.shape[2]),
        ),
    )
    interface = jnp.where(first_tile, padded_block, 0.0)
    rate_start = film_rate(film_m, film_halo(film_m), film_anis, interface)
    predicted = film_m + time_step * rate_start
    rate_trial = film_rate(predicted, film_halo(predicted), film_anis, interface)
    corrected = film_m + 0.5 * time_step * (rate_start + rate_trial)
    return (stack_spins, normalized(corrected))


LANES = 128
EDGE = 8
ROUNDS = 2 * SWEEPS
MESH = pl.DeviceIdType.MESH


def kernel_fits(spins, film_m, counts):
    _, gx_count, gy_count = counts
    _, _, rows_x, rows_y = spins.shape
    cells_x, cells_y = rows_x // K * gx_count, rows_y // K * gy_count
    return (
        rows_y == LANES
        and rows_x % 16 == 0
        and EDGE % (rows_x // K) == 0
        and cells_x % EDGE == 0
        and 3 * cells_y <= LANES
        and 3 * (rows_x // K) <= 16
        and film_m.shape[1] % 16 == 0
        and cells_x + 16 <= film_m.shape[1]
        and film_m.shape[2] % LANES == 0
        and cells_y + 2 <= film_m.shape[2]
        and 3 * spins.shape[1] <= EDGE
    )


def unit(vector):
    scale = lax.rsqrt(vector[0] * vector[0] + vector[1] * vector[1] + vector[2] * vector[2])
    return [part * scale for part in vector]


def cross(left, right):
    return [
        left[1] * right[2] - left[2] * right[1],
        left[2] * right[0] - left[0] * right[2],
        left[0] * right[1] - left[1] * right[0],
    ]


def fused_kernel(
    counts,
    exch,
    spins_hbm,
    unif_hbm,
    trial_hbm,
    film_hbm,
    anis_hbm,
    spins_out,
    film_out,
    stack,
    unif,
    trial,
    film_near,
    film,
    trial_film,
    half_film,
    anis,
    x_send,
    x_recv,
    y_send,
    y_recv,
    z_recv,
    fx_send,
    fx_recv,
    fy_send,
    fy_recv,
    cell_all,
    cell_own,
    cell_wide,
    mean_send,
    mean_recv,
    inter,
    local_sem,
    send_sem,
    recv_sem,
    film_send_sem,
    film_recv_sem,
    block_send_sem,
    block_recv_sem,
    cell_send_sem,
    cell_recv_sem,
    mean_send_sem,
    mean_recv_sem,
):
    regions, gx_count, gy_count = counts
    layers, rows = spins_hbm.shape[1], spins_hbm.shape[2]
    film_rows, film_cols = film_hbm.shape[1], film_hbm.shape[2]
    piece_x, piece_y = rows // K, LANES // K
    cells_x, cells_y = piece_x * gx_count, piece_y * gy_count
    per_tile = EDGE // piece_x
    inner = pl.ds(EDGE, rows)
    film_inner = pl.ds(EDGE, film_rows)
    region = lax.axis_index("region")
    gx = lax.axis_index("gx")
    gy = lax.axis_index("gy")
    first = (region == 0) & (gx == 0) & (gy == 0)
    not_first = jnp.logical_not(first)
    leader = (gx == 0) & (gy == 0)

    places = [
        (region > 0, (region - 1, gx, gy)),
        (region < regions - 1, (region + 1, gx, gy)),
        (gx > 0, (region, gx - 1, gy)),
        (gx < gx_count - 1, (region, gx + 1, gy)),
        (gy > 0, (region, gx, gy - 1)),
        (gy < gy_count - 1, (region, gx, gy + 1)),
    ]
    line = region * gx_count + gx
    film_places = [
        (line > 0, ((line + gx_count * regions - 1) // gx_count % regions, (gx + gx_count - 1) % gx_count, gy)),
        (line < regions * gx_count - 1, ((line + 1) // gx_count % regions, (gx + 1) % gx_count, gy)),
        places[4],
        places[5],
    ]

    loads = [
        pltpu.make_async_copy(source, target, local_sem.at[at])
        for at, (source, target) in enumerate(
            [
                (spins_hbm, stack.at[0, :, :, inner, :]),
                (film_hbm, film.at[:, film_inner, :]),
                (trial_hbm, trial),
                (unif_hbm, unif),
                (anis_hbm, anis),
            ]
        )
    ]
    for load in loads:
        load.start()

    barrier = pltpu.get_barrier_semaphore()
    for there, place in places + film_places[:2]:

        @pl.when(there)
        def _(place=place):
            pl.semaphore_signal(barrier, inc=1, device_id=place, device_id_type=MESH)

    @pl.when(jnp.logical_not(leader))
    def _():
        pl.semaphore_signal(barrier, inc=1, device_id=(region, 0, 0), device_id_type=MESH)

    @pl.when(leader & not_first)
    def _():
        pl.semaphore_signal(barrier, inc=1, device_id=(0, 0, 0), device_id_type=MESH)

    @pl.when(first)
    def _():
        for gx_at in range(gx_count):
            for gy_at in range(gy_count):
                if gx_at or gy_at:
                    pl.semaphore_signal(barrier, inc=1, device_id=(0, gx_at, gy_at), device_id_type=MESH)

    lane = lax.broadcasted_iota(jnp.int32, (rows, LANES), 1)
    film_lane = lax.broadcasted_iota(jnp.int32, (film_rows, LANES), 1)

    def halo(turn, way):
        if way < 2:
            source = stack.at[turn, :, 0 if way == 0 else layers - 1, inner, :]
            return source, z_recv
        if way < 4:
            return x_send.at[turn, way - 2], x_recv
        return y_send.at[turn, way - 4], y_recv

    def halo_copy(turn, way, slot):
        source, target = halo(turn, way)
        return pltpu.make_async_remote_copy(
            src_ref=source,
            dst_ref=target.at[turn, slot % 2],
            send_sem=send_sem.at[turn, way],
            recv_sem=recv_sem.at[turn, slot],
            device_id=places[way][1],
            device_id_type=MESH,
        )

    def film_copy(turn, way, slot):
        source, target = (fx_send, fx_recv) if way < 2 else (fy_send, fy_recv)
        return pltpu.make_async_remote_copy(
            src_ref=source.at[turn, way % 2],
            dst_ref=target.at[turn, slot % 2],
            send_sem=film_send_sem.at[turn, way],
            recv_sem=film_recv_sem.at[turn, slot],
            device_id=film_places[way][1],
            device_id_type=MESH,
        )

    def pack_halo(turn):
        right = jnp.zeros((rows, LANES), jnp.float32)
        left = right
        for part in range(3):
            for layer in range(layers):
                at = part * layers + layer
                block = stack[turn, part, layer, inner, :]
                x_send[turn, 0, at : at + 1, :] = stack[turn, part, layer, EDGE : EDGE + 1, :]
                x_send[turn, 1, at : at + 1, :] = stack[turn, part, layer, EDGE + rows - 1 : EDGE + rows, :]
                left = jnp.where(lane == at, pltpu.roll(block, at, 1) if at else block, left)
                right = jnp.where(lane == at, pltpu.roll(block, at + 1, 1), right)
        y_send[turn, 0] = left
        y_send[turn, 1] = right

    def send_halo(turn, ways):
        for way in ways:

            @pl.when(places[way][0])
            def _(way=way):
                halo_copy(turn, way, way ^ 1).start()

    def take_halo(turn):
        for way in range(6):

            @pl.when(places[way][0])
            def _(way=way):
                halo_copy(turn, way, way).wait_recv()

        for part in range(3):
            for layer in range(layers):
                at = part * layers + layer
                stack[turn, part, layer, EDGE - 1 : EDGE, :] = x_recv[turn, 0, at : at + 1, :]
                stack[turn, part, layer, EDGE + rows : EDGE + rows + 1, :] = x_recv[turn, 1, at : at + 1, :]

    def pack_film(turn, source):
        left = jnp.zeros((film_rows, LANES), jnp.float32)
        right = left
        for part in range(3):
            fx_send[turn, 0, part : part + 1, :] = source[part, EDGE : EDGE + 1, :]
            fx_send[turn, 1, part : part + 1, :] = source[part, EDGE + film_rows - 1 : EDGE + film_rows, :]
            head = source[part, film_inner, :LANES]
            tail = source[part, film_inner, film_cols - LANES :]
            left = jnp.where(film_lane == part, pltpu.roll(head, part, 1) if part else head, left)
            right = jnp.where(film_lane == part, pltpu.roll(tail, part + 1, 1), right)
        fy_send[turn, 0] = left
        fy_send[turn, 1] = right

    def send_film(turn):
        for way in range(4):

            @pl.when(film_places[way][0])
            def _(way=way):
                film_copy(turn, way, way ^ 1).start()

    def take_film(turn, target):
        for way in range(4):

            @pl.when(film_places[way][0])
            def _(way=way):
                film_copy(turn, way, way).wait_recv()

        for part in range(3):
            target[part, EDGE - 1 : EDGE, :] = fx_recv[turn, 0, part : part + 1, :]
            target[part, EDGE + film_rows : EDGE + film_rows + 1, :] = fx_recv[turn, 1, part : part + 1, :]

    def rate(turn, source, low, count, with_inter):
        wide = lax.broadcasted_iota(jnp.int32, (count, film_cols), 1)
        repeat = film_cols // LANES
        magnet, field = [], []
        for part in range(3):
            at = EDGE + low
            block = source[part, at : at + count, :]
            before = pltpu.roll(fy_recv[turn, 0, low : low + count, :], (LANES - part) % LANES, 1) if part else fy_recv[turn, 0, low : low + count, :]
            after = pltpu.roll(fy_recv[turn, 1, low : low + count, :], LANES - 1 - part, 1)
            total = source[part, at - 1 : at - 1 + count, :] + source[part, at + 1 : at + 1 + count, :]
            total = total + jnp.where(wide == 0, jnp.concatenate([before] * repeat, 1), pltpu.roll(block, 1, 1))
            total = total + jnp.where(
                wide == film_cols - 1, jnp.concatenate([after] * repeat, 1), pltpu.roll(block, film_cols - 1, 1)
            )
            total = total - 4.0 * block
            if with_inter:
                extra = coupling_up * inter[part, low : low + count, :]
                rest = [jnp.zeros((count, LANES), jnp.float32)] * (repeat - 1)
                total = total + jnp.concatenate([extra] + rest, 1)
            magnet.append(block)
            field.append(total)
        field[2] = field[2] + anis[low : low + count, :] * magnet[2]
        precession = cross(magnet, field)
        relaxation = cross(magnet, precession)
        factor = -1.0 / (1.0 + damping * damping)
        return magnet, [factor * (one + damping * two) for one, two in zip(precession, relaxation)]

    def film_start(low, count, with_inter=False):
        magnet, speed = rate(0, film, low, count, with_inter)
        for part in range(3):
            trial_film[part, EDGE + low : EDGE + low + count, :] = magnet[part] + time_step * speed[part]
            half_film[part, low : low + count, :] = magnet[part] + (0.5 * time_step) * speed[part]

    def film_end(low, count, with_inter=False):
        _, speed = rate(1, trial_film, low, count, with_inter)
        result = unit([half_film[part, low : low + count, :] + (0.5 * time_step) * speed[part] for part in range(3)])
        for part in range(3):
            film_out[part, low : low + count, :] = result[part]

    x_iota = lax.broadcasted_iota(jnp.int32, (rows, LANES), 0)

    def half_sweep(turn, send_mean):
        sweep, colour = turn // 2, turn % 2
        for layer in range(layers):
            own = [stack[turn, part, layer, inner, :] for part in range(3)]
            proposal = unit([own[part] + step_cone * trial[sweep, part, layer] for part in range(3)])
            around = [[] for _ in range(6)]
            for part in range(3):
                at = part * layers + layer
                around[0].append(z_recv[turn, 0, part] if layer == 0 else stack[turn, part, layer - 1, inner, :])
                around[1].append(z_recv[turn, 1, part] if layer == layers - 1 else stack[turn, part, layer + 1, inner, :])
                around[2].append(stack[turn, part, layer, EDGE - 1 : EDGE - 1 + rows, :])
                around[3].append(stack[turn, part, layer, EDGE + 1 : EDGE + 1 + rows, :])
                before = pltpu.roll(y_recv[turn, 0], LANES - at, 1) if at else y_recv[turn, 0]
                after = pltpu.roll(y_recv[turn, 1], LANES - 1 - at, 1)
                around[4].append(jnp.where(lane == 0, before, pltpu.roll(own[part], 1, 1)))
                around[5].append(jnp.where(lane == LANES - 1, after, pltpu.roll(own[part], LANES - 1, 1)))
            gain = jnp.zeros((rows, LANES), jnp.float32)
            shift = [proposal[part] - own[part] for part in range(3)]
            for part in range(3):
                field = coupling_down * film_near[part]
                for way in range(3):
                    for other in range(3):
                        field = field + exch[way, part, other] * around[2 * way + 1][other]
                        field = field + exch[way, other, part] * around[2 * way][other]
                gain = gain + shift[part] * field
            change = -gain - anisotropy * (proposal[2] * proposal[2] - own[2] * own[2])
            accept = jnp.exp(jnp.minimum(-inverse_temp * change, 0.0))
            weight = 1.0 / (1.0 + jnp.exp((unif[sweep, layer] - accept) * (1.0 / softness)))
            blended = unit([own[part] + weight * shift[part] for part in range(3)])
            parity = (region * layers + layer + gx * rows + gy * LANES + x_iota + lane) % 2
            for part in range(3):
                fresh = jnp.where(parity == colour, blended[part], own[part])
                if turn == ROUNDS - 1:
                    spins_out[part, layer] = fresh
                else:
                    stack[turn + 1, part, layer, inner, :] = fresh
            if turn == ROUNDS - 1:
                if layer == 0:
                    send_mean()
            else:
                if layer == 0:
                    send_halo(turn + 1, [0])
                if layer == layers - 1:
                    send_halo(turn + 1, [1])

    def block_copy(region_at):
        return pltpu.make_async_remote_copy(
            src_ref=cell_all,
            dst_ref=cell_all,
            send_sem=block_send_sem.at[region_at],
            recv_sem=block_recv_sem,
            device_id=(region_at, 0, 0),
            device_id_type=MESH,
        )

    def cell_copy(gx_at, gy_at):
        return pltpu.make_async_remote_copy(
            src_ref=cell_all.at[pl.ds(gx_at // per_tile * EDGE, EDGE), :],
            dst_ref=cell_own,
            send_sem=cell_send_sem.at[gx_at * gy_count + gy_at],
            recv_sem=cell_recv_sem,
            device_id=(region, gx_at, gy_at),
            device_id_type=MESH,
        )

    members = [
        (gx_at, gy_at)
        for gx_at in reversed(range(gx_count))
        for gy_at in reversed(range(gy_count))
        if gx_at or gy_at
    ]

    def mean_copy(gx_at, gy_at):
        number = gx_at * gy_count + gy_at
        return pltpu.make_async_remote_copy(
            src_ref=mean_send,
            dst_ref=mean_recv.at[number],
            send_sem=mean_send_sem,
            recv_sem=mean_recv_sem.at[number],
            device_id=(0, 0, 0),
            device_id_type=MESH,
        )

    for way in range(6):

        @pl.when(jnp.logical_not(places[way][0]))
        def _(way=way):
            for turn in range(ROUNDS):
                target = halo(turn, way)[1]
                target[turn, way % 2] = jnp.zeros(target.shape[2:], jnp.float32)

    for way in range(4):

        @pl.when(jnp.logical_not(film_places[way][0]))
        def _(way=way):
            target = fx_recv if way < 2 else fy_recv
            for turn in range(2):
                target[turn, way % 2] = jnp.zeros(target.shape[2:], jnp.float32)

    loads[0].wait()
    pack_halo(0)
    loads[1].wait()

    @pl.when(first)
    def _():
        cell_lane = lax.broadcasted_iota(jnp.int32, (cells_x, LANES), 1)
        packed = film[0, EDGE : EDGE + cells_x, :LANES]
        for part in (1, 2):
            moved = pltpu.roll(film[part, EDGE : EDGE + cells_x, :LANES], part * cells_y, 1)
            packed = jnp.where(cell_lane >= part * cells_y, moved, packed)
        cell_all[...] = packed

    pack_film(0, film)

    expected = sum(there.astype(jnp.int32) for there, _ in places + film_places[:2])
    expected = expected + jnp.where(leader, gx_count * gy_count - 1, jnp.where(region == 0, 1, 0))
    expected = expected + jnp.where(first, regions - 1, 0)
    pl.semaphore_wait(barrier, expected)

    @pl.when(first)
    def _():
        for region_at in reversed(range(1, regions)):
            block_copy(region_at).start()
        for member in members:
            cell_copy(*member).start()

    send_halo(0, range(6))
    send_film(0)

    @pl.when(leader & not_first)
    def _():
        block_copy(0).wait_recv()
        for member in members:
            cell_copy(*member).start()

    row_at = lax.broadcasted_iota(jnp.int32, (LANES, LANES), 0)
    col_at = lax.broadcasted_iota(jnp.int32, (LANES, LANES), 1)
    dot = functools.partial(jnp.dot, precision=lax.Precision.HIGHEST, preferred_element_type=jnp.float32)
    film_steps = list(range(0, film_rows, 16))
    for load in loads[2:]:
        load.wait()
    take_film(0, film)
    for low in film_steps:
        film_start(low, 16)
    pack_film(1, trial_film)
    send_film(1)

    @pl.when(leader)
    def _():
        cell_own[...] = cell_all[:EDGE, :]

    @pl.when(jnp.logical_not(leader))
    def _():
        cell_copy(0, 0).wait_recv()

    cells = cell_own[...]
    for part in range(3):
        spread_cols = (row_at == part * cells_y + gy * piece_y + col_at // K).astype(jnp.float32)
        cell_wide[part] = dot(cells, spread_cols)
    for part in range(3):
        for at in range(piece_x):
            line_at = cell_wide[part, pl.ds(gx % per_tile * piece_x + at, 1), :]
            film_near[part, at * K : (at + 1) * K, :] = jnp.broadcast_to(line_at, (K, LANES))

    def send_mean():
        @pl.when(region == 0)
        def _():
            for part in range(3):
                for at in range(piece_x):
                    block = spins_out[part, 0, at * K : (at + 1) * K, :]
                    place = part * piece_x + at
                    mean_send[place : place + 1, :] = jnp.sum(block, axis=0, keepdims=True)
            for at in range(3 * piece_x, 16):
                mean_send[at : at + 1, :] = jnp.zeros((1, LANES), jnp.float32)
            gather_cols = jnp.where(col_at == row_at // K + gy * piece_y, 1.0 / (K * K), 0.0)
            mean_send[...] = dot(mean_send[...], gather_cols)

            @pl.when(not_first)
            def _():
                number = gx * gy_count + gy
                pltpu.make_async_remote_copy(
                    src_ref=mean_send,
                    dst_ref=mean_recv.at[number],
                    send_sem=mean_send_sem,
                    recv_sem=mean_recv_sem.at[number],
                    device_id=(0, 0, 0),
                    device_id_type=MESH,
                ).start()

    half = len(film_steps) // 2
    for turn in range(ROUNDS):
        take_halo(turn)
        half_sweep(turn, send_mean)
        if turn + 1 < ROUNDS:
            pack_halo(turn + 1)
            send_halo(turn + 1, range(2, 6))
        if turn == 0:
            take_film(1, trial_film)
            for low in film_steps[:half]:
                film_end(low, 16)
        if turn == 1:
            for low in film_steps[half:]:
                film_end(low, 16)

    @pl.when(first)
    def _():
        inter[...] = jnp.zeros(inter.shape, jnp.float32)
        for gx_at in range(gx_count):
            total = jnp.zeros((16, LANES), jnp.float32)
            for gy_at in range(gy_count):
                if gx_at or gy_at:
                    mean_copy(gx_at, gy_at).wait_recv()
                    total = total + mean_recv[gx_at * gy_count + gy_at]
                else:
                    total = total + mean_send[...]
            for part in range(3):
                inter[part, gx_at * piece_x : (gx_at + 1) * piece_x, :] = total[
                    part * piece_x : (part + 1) * piece_x
                ]
        film_start(0, cells_x, True)
        film_end(0, cells_x + EDGE, True)
        for region_at in range(1, regions):
            block_copy(region_at).wait_send()

    @pl.when(leader)
    def _():
        for member in members:
            cell_copy(*member).wait_send()

    @pl.when((region == 0) & not_first)
    def _():
        mean_copy(0, 0).wait_send()

    for turn in range(ROUNDS):
        for way in range(6):

            @pl.when(places[way][0])
            def _(turn=turn, way=way):
                halo_copy(turn, way, way ^ 1).wait_send()

    for turn in range(2):
        for way in range(4):

            @pl.when(film_places[way][0])
            def _(turn=turn, way=way):
                film_copy(turn, way, way ^ 1).wait_send()


def body(spins, uniforms, trials, exch_kernel, film_m, film_anis):
    counts = tuple(lax.axis_size(axis) for axis in ("region", "gx", "gy"))
    if not kernel_fits(spins, film_m, counts):
        return body_general(spins, uniforms, trials, exch_kernel, film_m, film_anis)
    regions, gx_count, gy_count = counts
    _, layers, rows, _ = spins.shape
    _, film_rows, film_cols = film_m.shape
    cells_x = rows // K * gx_count
    tiles = gx_count * gy_count
    dma = pltpu.SemaphoreType.DMA

    def vmem(*shape):
        return pltpu.VMEM(shape, jnp.float32)

    anywhere = pl.BlockSpec(memory_space=pltpu.HBM)
    inside = pl.BlockSpec(memory_space=pltpu.VMEM)
    return pl.pallas_call(
        functools.partial(fused_kernel, counts),
        out_shape=(
            jax.ShapeDtypeStruct(spins.shape, jnp.float32),
            jax.ShapeDtypeStruct(film_m.shape, jnp.float32),
        ),
        in_specs=[pl.BlockSpec(memory_space=pltpu.SMEM)] + [anywhere] * 5,
        out_specs=(inside, inside),
        scratch_shapes=[
            vmem(ROUNDS, 3, layers, rows + 2 * EDGE, LANES),
            vmem(*uniforms.shape),
            vmem(*trials.shape),
            vmem(3, rows, LANES),
            vmem(3, film_rows + 2 * EDGE, film_cols),
            vmem(3, film_rows + 2 * EDGE, film_cols),
            vmem(3, film_rows, film_cols),
            vmem(film_rows, film_cols),
            vmem(ROUNDS, 2, EDGE, LANES),
            vmem(ROUNDS, 2, EDGE, LANES),
            vmem(ROUNDS, 2, rows, LANES),
            vmem(ROUNDS, 2, rows, LANES),
            vmem(ROUNDS, 2, 3, rows, LANES),
            vmem(2, 2, EDGE, film_cols),
            vmem(2, 2, EDGE, film_cols),
            vmem(2, 2, film_rows, LANES),
            vmem(2, 2, film_rows, LANES),
            vmem(cells_x, LANES),
            vmem(EDGE, LANES),
            vmem(3, EDGE, LANES),
            vmem(16, LANES),
            vmem(tiles, 16, LANES),
            vmem(3, cells_x + EDGE, LANES),
            dma((5,)),
            dma((ROUNDS, 6)),
            dma((ROUNDS, 6)),
            dma((2, 4)),
            dma((2, 4)),
            dma((regions,)),
            dma,
            dma((tiles,)),
            dma,
            dma,
            dma((tiles,)),
        ],
        compiler_params=pltpu.CompilerParams(
            collective_id=0, has_side_effects=True, vmem_limit_bytes=60 * 1024 * 1024
        ),
    )(exch_kernel, spins, uniforms, trials, film_m, film_anis)


def solution(mesh):
    return jax.shard_map(
        body,
        mesh=mesh,
        in_specs=(
            P(None, "region", "gx", "gy"),
            P(None, "region", "gx", "gy"),
            P(None, None, "region", "gx", "gy"),
            P(),
            P(None, ("region", "gx"), "gy"),
            P(("region", "gx"), "gy"),
        ),
        out_specs=(P(None, "region", "gx", "gy"), P(None, ("region", "gx"), "gy")),
        check_vma=False,
    )
```

```python
import functools

import jax
import jax.numpy as jnp
from jax import lax
from jax.experimental import pallas as pl
from jax.experimental.pallas import tpu as pltpu
from jax.sharding import PartitionSpec as P

K = 8
SWEEPS = 2


coupling_down = 1.0
anisotropy = 0.5
inverse_temp = 2.0
softness = 0.05
step_cone = 0.4
coupling_up = 2.0
damping = 0.1
time_step = 0.05


def extended(cells, sides, width):
    for axis, dim in sides:
        count = lax.axis_size(axis)
        ends = count - 1
        head = lax.slice_in_dim(cells, 0, width, axis=dim)
        tail = lax.slice_in_dim(cells, cells.shape[dim] - width, cells.shape[dim], axis=dim)
        cells = jnp.concatenate(
            [
                lax.ppermute(tail, axis, [(i, (i + 1) % count) for i in range(ends)]),
                cells,
                lax.ppermute(head, axis, [((i + 1) % count, i) for i in range(ends)]),
            ],
            axis=dim,
        )
    return cells


def spread(value, axis, source):
    kept = jnp.where(lax.axis_index(axis) == source, value, 0).astype(value.dtype)
    return lax.psum(kept, axis)


def normalized(vector):
    return vector / jnp.sqrt(jnp.sum(vector * vector, axis=0, keepdims=True))


def apply_kernel(matrix, vector):
    return jnp.stack(
        [
            matrix[component, 0] * vector[0]
            + matrix[component, 1] * vector[1]
            + matrix[component, 2] * vector[2]
            for component in range(3)
        ]
    )


def apply_transposed(matrix, vector):
    return jnp.stack(
        [
            matrix[0, component] * vector[0]
            + matrix[1, component] * vector[1]
            + matrix[2, component] * vector[2]
            for component in range(3)
        ]
    )


def local_field(padded, exch_kernel):
    forward = (padded[:, 2:, 1:-1, 1:-1], padded[:, 1:-1, 2:, 1:-1], padded[:, 1:-1, 1:-1, 2:])
    backward = (padded[:, :-2, 1:-1, 1:-1], padded[:, 1:-1, :-2, 1:-1], padded[:, 1:-1, 1:-1, :-2])
    summed = apply_kernel(exch_kernel[0], forward[0]) + apply_transposed(
        exch_kernel[0], backward[0]
    )
    for direction in (1, 2):
        summed = summed + apply_kernel(exch_kernel[direction], forward[direction])
        summed = summed + apply_transposed(exch_kernel[direction], backward[direction])
    return summed


def metropolis(spins, padded, exch_kernel, film_near, trial_move, uniform_draw, colour_mask):
    field_sum = local_field(padded, exch_kernel) + coupling_down * film_near
    proposal = normalized(spins + step_cone * trial_move)
    change = -jnp.sum((proposal - spins) * field_sum, axis=0) - anisotropy * (
        proposal[2] * proposal[2] - spins[2] * spins[2]
    )
    accept = jnp.exp(jnp.minimum(-inverse_temp * change, 0.0))
    weight = jax.nn.sigmoid((accept - uniform_draw) / softness)
    blended = normalized((1.0 - weight) * spins + weight * proposal)
    return jnp.where(colour_mask[None], blended, spins)


def cross_product(left, right):
    return jnp.stack(
        [
            left[1] * right[2] - left[2] * right[1],
            left[2] * right[0] - left[0] * right[2],
            left[0] * right[1] - left[1] * right[0],
        ]
    )


def film_rate(magnet, padded, film_anis, interface):
    laplace_sum = (
        padded[:, 2:, 1:-1]
        + padded[:, :-2, 1:-1]
        + padded[:, 1:-1, 2:]
        + padded[:, 1:-1, :-2]
        - 4.0 * magnet
    )
    field_sum = laplace_sum + coupling_up * interface
    field_sum = jnp.stack([field_sum[0], field_sum[1], field_sum[2] + film_anis * magnet[2]])
    precession = cross_product(magnet, field_sum)
    relaxation = cross_product(magnet, precession)
    return -(precession + damping * relaxation) / (1.0 + damping * damping)


def film_halo(magnet):
    return extended(magnet, ((("region", "gx"), 1), ("gy", 2)), 1)


def body_general(spins, uniforms, trials, exch_kernel, film_m, film_anis):
    layers_dev = spins.shape[1]
    rows_x = spins.shape[2]
    rows_y = spins.shape[3]
    piece_x = rows_x // K
    piece_y = rows_y // K
    gx_count = lax.axis_size("gx")
    gy_count = lax.axis_size("gy")
    region_pos = lax.axis_index("region")
    gx_pos = lax.axis_index("gx")
    gy_pos = lax.axis_index("gy")
    first_tile = (region_pos == 0) & (gx_pos == 0) & (gy_pos == 0)
    film_block = film_m[:, : piece_x * gx_count, : piece_y * gy_count]
    stack_spins, unif_all, trial_all = (spins, uniforms, trials)
    layer_pos = region_pos * layers_dev + jnp.arange(layers_dev, dtype=jnp.int32)
    film_block = spread(film_block, ("region", "gx", "gy"), 0)
    own_cells = lax.dynamic_slice(
        film_block, (jnp.int32(0), gx_pos * piece_x, gy_pos * piece_y), (3, piece_x, piece_y)
    )
    film_cells = jnp.repeat(jnp.repeat(own_cells, K, axis=1), K, axis=2)
    film_near = jnp.broadcast_to(film_cells[:, None], (3, stack_spins.shape[1], rows_x, rows_y))
    x_global = gx_pos * rows_x + jnp.arange(rows_x, dtype=jnp.int32)
    y_global = gy_pos * rows_y + jnp.arange(rows_y, dtype=jnp.int32)
    parity = (layer_pos[:, None, None] + x_global[None, :, None] + y_global[None, None, :]) % 2
    for sweep_index in range(SWEEPS):
        for colour in (0, 1):
            padded = extended(stack_spins, (("region", 1), ("gx", 2), ("gy", 3)), 1)
            stack_spins = metropolis(
                stack_spins,
                padded,
                exch_kernel,
                film_near,
                trial_all[sweep_index],
                unif_all[sweep_index],
                parity == colour,
            )
    averages = stack_spins[:, 0].reshape(3, piece_x, K, piece_y, K).mean(axis=(2, 4))
    gathered = lax.all_gather(averages[None], ("gx", "gy"), axis=0, tiled=True)
    assembled = (
        gathered.reshape(gx_count, gy_count, 3, piece_x, piece_y)
        .transpose(2, 0, 3, 1, 4)
        .reshape(3, gx_count * piece_x, gy_count * piece_y)
    )
    padded_block = jnp.pad(
        assembled,
        (
            (0, 0),
            (0, film_m.shape[1] - assembled.shape[1]),
            (0, film_m.shape[2] - assembled.shape[2]),
        ),
    )
    interface = jnp.where(first_tile, padded_block, 0.0)
    rate_start = film_rate(film_m, film_halo(film_m), film_anis, interface)
    predicted = film_m + time_step * rate_start
    rate_trial = film_rate(predicted, film_halo(predicted), film_anis, interface)
    corrected = film_m + 0.5 * time_step * (rate_start + rate_trial)
    return (stack_spins, normalized(corrected))


LANES = 128
EDGE = 8
ROUNDS = 2 * SWEEPS
MESH = pl.DeviceIdType.MESH


def kernel_fits(spins, film_m, counts):
    _, gx_count, gy_count = counts
    _, _, rows_x, rows_y = spins.shape
    cells_x, cells_y = rows_x // K * gx_count, rows_y // K * gy_count
    return (
        rows_y == LANES
        and rows_x % 16 == 0
        and EDGE % (rows_x // K) == 0
        and cells_x % EDGE == 0
        and 3 * cells_y <= LANES
        and 3 * (rows_x // K) <= 16
        and film_m.shape[1] % 16 == 0
        and cells_x + 16 <= film_m.shape[1]
        and film_m.shape[2] % LANES == 0
        and cells_y + 2 <= film_m.shape[2]
        and 3 * spins.shape[1] <= EDGE
    )


def unit(vector):
    scale = lax.rsqrt(vector[0] * vector[0] + vector[1] * vector[1] + vector[2] * vector[2])
    return [part * scale for part in vector]


def cross(left, right):
    return [
        left[1] * right[2] - left[2] * right[1],
        left[2] * right[0] - left[0] * right[2],
        left[0] * right[1] - left[1] * right[0],
    ]


def fused_kernel(
    counts,
    exch,
    spins_hbm,
    unif_hbm,
    trial_hbm,
    film_hbm,
    anis_hbm,
    spins_out,
    film_out,
    stack,
    unif,
    trial,
    film_near,
    film,
    trial_film,
    half_film,
    anis,
    x_send,
    x_recv,
    y_send,
    y_recv,
    z_recv,
    fx_send,
    fx_recv,
    fy_send,
    fy_recv,
    cell_all,
    cell_own,
    cell_wide,
    mean_send,
    mean_recv,
    inter,
    local_sem,
    send_sem,
    recv_sem,
    film_send_sem,
    film_recv_sem,
    block_send_sem,
    block_recv_sem,
    cell_send_sem,
    cell_recv_sem,
    mean_send_sem,
    mean_recv_sem,
):
    regions, gx_count, gy_count = counts
    layers, rows = spins_hbm.shape[1], spins_hbm.shape[2]
    film_rows, film_cols = film_hbm.shape[1], film_hbm.shape[2]
    piece_x, piece_y = rows // K, LANES // K
    cells_x, cells_y = piece_x * gx_count, piece_y * gy_count
    per_tile = EDGE // piece_x
    inner = pl.ds(EDGE, rows)
    film_inner = pl.ds(EDGE, film_rows)
    region = lax.axis_index("region")
    gx = lax.axis_index("gx")
    gy = lax.axis_index("gy")
    first = (region == 0) & (gx == 0) & (gy == 0)
    not_first = jnp.logical_not(first)
    leader = (gx == 0) & (gy == 0)

    places = [
        (region > 0, (region - 1, gx, gy)),
        (region < regions - 1, (region + 1, gx, gy)),
        (gx > 0, (region, gx - 1, gy)),
        (gx < gx_count - 1, (region, gx + 1, gy)),
        (gy > 0, (region, gx, gy - 1)),
        (gy < gy_count - 1, (region, gx, gy + 1)),
    ]
    line = region * gx_count + gx
    film_places = [
        (line > 0, ((line + gx_count * regions - 1) // gx_count % regions, (gx + gx_count - 1) % gx_count, gy)),
        (line < regions * gx_count - 1, ((line + 1) // gx_count % regions, (gx + 1) % gx_count, gy)),
        places[4],
        places[5],
    ]

    loads = [
        pltpu.make_async_copy(source, target, local_sem.at[at])
        for at, (source, target) in enumerate(
            [
                (spins_hbm, stack.at[0, :, :, inner, :]),
                (film_hbm, film.at[:, film_inner, :]),
                (trial_hbm, trial),
                (unif_hbm, unif),
                (anis_hbm, anis),
            ]
        )
    ]
    for load in loads:
        load.start()

    barrier = pltpu.get_barrier_semaphore()
    for there, place in places + film_places[:2]:

        @pl.when(there)
        def _(place=place):
            pl.semaphore_signal(barrier, inc=1, device_id=place, device_id_type=MESH)

    @pl.when(jnp.logical_not(leader))
    def _():
        pl.semaphore_signal(barrier, inc=1, device_id=(region, 0, 0), device_id_type=MESH)

    @pl.when(leader & not_first)
    def _():
        pl.semaphore_signal(barrier, inc=1, device_id=(0, 0, 0), device_id_type=MESH)

    @pl.when(first)
    def _():
        for gx_at in range(gx_count):
            for gy_at in range(gy_count):
                if gx_at or gy_at:
                    pl.semaphore_signal(barrier, inc=1, device_id=(0, gx_at, gy_at), device_id_type=MESH)

    lane = lax.broadcasted_iota(jnp.int32, (rows, LANES), 1)
    film_lane = lax.broadcasted_iota(jnp.int32, (film_rows, LANES), 1)

    def halo(turn, way):
        if way < 2:
            source = stack.at[turn, :, 0 if way == 0 else layers - 1, inner, :]
            return source, z_recv
        if way < 4:
            return x_send.at[turn, way - 2], x_recv
        return y_send.at[turn, way - 4], y_recv

    def halo_copy(turn, way, slot):
        source, target = halo(turn, way)
        return pltpu.make_async_remote_copy(
            src_ref=source,
            dst_ref=target.at[turn, slot % 2],
            send_sem=send_sem.at[turn, way],
            recv_sem=recv_sem.at[turn, slot],
            device_id=places[way][1],
            device_id_type=MESH,
        )

    def film_copy(turn, way, slot):
        source, target = (fx_send, fx_recv) if way < 2 else (fy_send, fy_recv)
        return pltpu.make_async_remote_copy(
            src_ref=source.at[turn, way % 2],
            dst_ref=target.at[turn, slot % 2],
            send_sem=film_send_sem.at[turn, way],
            recv_sem=film_recv_sem.at[turn, slot],
            device_id=film_places[way][1],
            device_id_type=MESH,
        )

    def pack_halo(turn):
        right = jnp.zeros((rows, LANES), jnp.float32)
        left = right
        for part in range(3):
            for layer in range(layers):
                at = part * layers + layer
                block = stack[turn, part, layer, inner, :]
                x_send[turn, 0, at : at + 1, :] = stack[turn, part, layer, EDGE : EDGE + 1, :]
                x_send[turn, 1, at : at + 1, :] = stack[turn, part, layer, EDGE + rows - 1 : EDGE + rows, :]
                left = jnp.where(lane == at, pltpu.roll(block, at, 1) if at else block, left)
                right = jnp.where(lane == at, pltpu.roll(block, at + 1, 1), right)
        y_send[turn, 0] = left
        y_send[turn, 1] = right

    def send_halo(turn, ways):
        for way in ways:

            @pl.when(places[way][0])
            def _(way=way):
                halo_copy(turn, way, way ^ 1).start()

    def take_halo(turn):
        for way in range(6):

            @pl.when(places[way][0])
            def _(way=way):
                halo_copy(turn, way, way).wait_recv()

        for part in range(3):
            for layer in range(layers):
                at = part * layers + layer
                stack[turn, part, layer, EDGE - 1 : EDGE, :] = x_recv[turn, 0, at : at + 1, :]
                stack[turn, part, layer, EDGE + rows : EDGE + rows + 1, :] = x_recv[turn, 1, at : at + 1, :]

    def pack_film(turn, source):
        left = jnp.zeros((film_rows, LANES), jnp.float32)
        right = left
        for part in range(3):
            fx_send[turn, 0, part : part + 1, :] = source[part, EDGE : EDGE + 1, :]
            fx_send[turn, 1, part : part + 1, :] = source[part, EDGE + film_rows - 1 : EDGE + film_rows, :]
            head = source[part, film_inner, :LANES]
            tail = source[part, film_inner, film_cols - LANES :]
            left = jnp.where(film_lane == part, pltpu.roll(head, part, 1) if part else head, left)
            right = jnp.where(film_lane == part, pltpu.roll(tail, part + 1, 1), right)
        fy_send[turn, 0] = left
        fy_send[turn, 1] = right

    def send_film(turn):
        for way in range(4):

            @pl.when(film_places[way][0])
            def _(way=way):
                film_copy(turn, way, way ^ 1).start()

    def take_film(turn, target):
        for way in range(4):

            @pl.when(film_places[way][0])
            def _(way=way):
                film_copy(turn, way, way).wait_recv()

        for part in range(3):
            target[part, EDGE - 1 : EDGE, :] = fx_recv[turn, 0, part : part + 1, :]
            target[part, EDGE + film_rows : EDGE + film_rows + 1, :] = fx_recv[turn, 1, part : part + 1, :]

    def rate(turn, source, low, count, with_inter):
        wide = lax.broadcasted_iota(jnp.int32, (count, film_cols), 1)
        repeat = film_cols // LANES
        magnet, field = [], []
        for part in range(3):
            tall = source[part, pl.ds(low, count + 2 * EDGE), :]
            span = count + 2 * EDGE
            block = tall[EDGE : EDGE + count]
            before = fy_recv[turn, 0, pl.ds(low, count), :]
            before = pltpu.roll(before, LANES - part, 1) if part else before
            after = pltpu.roll(fy_recv[turn, 1, pl.ds(low, count), :], LANES - 1 - part, 1)
            total = (pltpu.roll(tall, 1, 0) + pltpu.roll(tall, span - 1, 0))[EDGE : EDGE + count]
            total = total + jnp.where(wide == 0, jnp.concatenate([before] * repeat, 1), pltpu.roll(block, 1, 1))
            total = total + jnp.where(
                wide == film_cols - 1, jnp.concatenate([after] * repeat, 1), pltpu.roll(block, film_cols - 1, 1)
            )
            total = total - 4.0 * block
            if with_inter:
                extra = coupling_up * inter[part, pl.ds(low, count), :]
                rest = [jnp.zeros((count, LANES), jnp.float32)] * (repeat - 1)
                total = total + jnp.concatenate([extra] + rest, 1)
            magnet.append(block)
            field.append(total)
        field[2] = field[2] + anis[pl.ds(low, count), :] * magnet[2]
        precession = cross(magnet, field)
        relaxation = cross(magnet, precession)
        factor = -1.0 / (1.0 + damping * damping)
        return magnet, [factor * (one + damping * two) for one, two in zip(precession, relaxation)]

    def film_start(low, count, with_inter=False):
        magnet, speed = rate(0, film, low, count, with_inter)
        for part in range(3):
            trial_film[part, pl.ds(low + EDGE, count), :] = magnet[part] + time_step * speed[part]
            half_film[part, pl.ds(low, count), :] = magnet[part] + (0.5 * time_step) * speed[part]

    def film_end(low, count, with_inter=False):
        _, speed = rate(1, trial_film, low, count, with_inter)
        result = unit([half_film[part, pl.ds(low, count), :] + (0.5 * time_step) * speed[part] for part in range(3)])
        for part in range(3):
            film_out[part, pl.ds(low, count), :] = result[part]

    x_iota = lax.broadcasted_iota(jnp.int32, (rows, LANES), 0)

    def half_sweep(turn, send_mean, last):
        sweep, colour = turn // 2, turn % 2
        for layer in range(layers):
            own = [stack[turn, part, layer, inner, :] for part in range(3)]
            proposal = unit([own[part] + step_cone * trial[sweep, part, layer] for part in range(3)])
            around = [[] for _ in range(6)]
            for part in range(3):
                at = part * layers + layer
                around[0].append(z_recv[turn, 0, part] if layer == 0 else stack[turn, part, layer - 1, inner, :])
                around[1].append(z_recv[turn, 1, part] if layer == layers - 1 else stack[turn, part, layer + 1, inner, :])
                around[2].append(stack[turn, part, layer, EDGE - 1 : EDGE - 1 + rows, :])
                around[3].append(stack[turn, part, layer, EDGE + 1 : EDGE + 1 + rows, :])
                before = pltpu.roll(y_recv[turn, 0], LANES - at, 1) if at else y_recv[turn, 0]
                after = pltpu.roll(y_recv[turn, 1], LANES - 1 - at, 1)
                around[4].append(jnp.where(lane == 0, before, pltpu.roll(own[part], 1, 1)))
                around[5].append(jnp.where(lane == LANES - 1, after, pltpu.roll(own[part], LANES - 1, 1)))
            gain = jnp.zeros((rows, LANES), jnp.float32)
            shift = [proposal[part] - own[part] for part in range(3)]
            for part in range(3):
                field = coupling_down * film_near[part]
                for way in range(3):
                    for other in range(3):
                        field = field + exch[way, part, other] * around[2 * way + 1][other]
                        field = field + exch[way, other, part] * around[2 * way][other]
                gain = gain + shift[part] * field
            change = -gain - anisotropy * (proposal[2] * proposal[2] - own[2] * own[2])
            accept = jnp.exp(jnp.minimum(-inverse_temp * change, 0.0))
            weight = 1.0 / (1.0 + jnp.exp((unif[sweep, layer] - accept) * (1.0 / softness)))
            blended = unit([own[part] + weight * shift[part] for part in range(3)])
            parity = (region * layers + layer + gx * rows + gy * LANES + x_iota + lane) % 2
            for part in range(3):
                fresh = jnp.where(parity == colour, blended[part], own[part])
                if last:
                    spins_out[part, layer] = fresh
                else:
                    stack[turn + 1, part, layer, inner, :] = fresh
            if last:
                if layer == 0:
                    send_mean()
            else:
                if layer == 0:
                    send_halo(turn + 1, [0])
                if layer == layers - 1:
                    send_halo(turn + 1, [1])

    def block_copy(region_at):
        return pltpu.make_async_remote_copy(
            src_ref=cell_all,
            dst_ref=cell_all,
            send_sem=block_send_sem.at[region_at],
            recv_sem=block_recv_sem,
            device_id=(region_at, 0, 0),
            device_id_type=MESH,
        )

    def cell_copy(gx_at, gy_at):
        return pltpu.make_async_remote_copy(
            src_ref=cell_all.at[pl.ds(gx_at // per_tile * EDGE, EDGE), :],
            dst_ref=cell_own,
            send_sem=cell_send_sem.at[gx_at * gy_count + gy_at],
            recv_sem=cell_recv_sem,
            device_id=(region, gx_at, gy_at),
            device_id_type=MESH,
        )

    members = [
        (gx_at, gy_at)
        for gx_at in reversed(range(gx_count))
        for gy_at in reversed(range(gy_count))
        if gx_at or gy_at
    ]

    def mean_copy(gx_at, gy_at):
        number = gx_at * gy_count + gy_at
        return pltpu.make_async_remote_copy(
            src_ref=mean_send,
            dst_ref=mean_recv.at[number],
            send_sem=mean_send_sem,
            recv_sem=mean_recv_sem.at[number],
            device_id=(0, 0, 0),
            device_id_type=MESH,
        )

    for way in range(6):

        @pl.when(jnp.logical_not(places[way][0]))
        def _(way=way):
            for turn in range(ROUNDS):
                target = halo(turn, way)[1]
                target[turn, way % 2] = jnp.zeros(target.shape[2:], jnp.float32)

    for way in range(4):

        @pl.when(jnp.logical_not(film_places[way][0]))
        def _(way=way):
            target = fx_recv if way < 2 else fy_recv
            for turn in range(2):
                target[turn, way % 2] = jnp.zeros(target.shape[2:], jnp.float32)

    loads[0].wait()
    pack_halo(0)
    loads[1].wait()

    @pl.when(first)
    def _():
        cell_lane = lax.broadcasted_iota(jnp.int32, (cells_x, LANES), 1)
        packed = film[0, EDGE : EDGE + cells_x, :LANES]
        for part in (1, 2):
            moved = pltpu.roll(film[part, EDGE : EDGE + cells_x, :LANES], part * cells_y, 1)
            packed = jnp.where(cell_lane >= part * cells_y, moved, packed)
        cell_all[...] = packed

    pack_film(0, film)

    expected = sum(there.astype(jnp.int32) for there, _ in places + film_places[:2])
    expected = expected + jnp.where(leader, gx_count * gy_count - 1, jnp.where(region == 0, 1, 0))
    expected = expected + jnp.where(first, regions - 1, 0)
    pl.semaphore_wait(barrier, expected)

    @pl.when(first)
    def _():
        for region_at in reversed(range(1, regions)):
            block_copy(region_at).start()
        for member in members:
            cell_copy(*member).start()

    send_halo(0, range(6))
    send_film(0)

    @pl.when(leader & not_first)
    def _():
        block_copy(0).wait_recv()
        for member in members:
            cell_copy(*member).start()

    row_at = lax.broadcasted_iota(jnp.int32, (LANES, LANES), 0)
    col_at = lax.broadcasted_iota(jnp.int32, (LANES, LANES), 1)
    dot = functools.partial(jnp.dot, precision=lax.Precision.HIGHEST, preferred_element_type=jnp.float32)
    film_steps = film_rows // 16

    def film_run(step, start, stop):
        def one(at, carry):
            step(pl.multiple_of(at * 16, 16), 16)
            return carry

        lax.fori_loop(start, stop, one, 0)

    for load in loads[2:]:
        load.wait()
    take_film(0, film)
    film_run(film_start, 0, film_steps)
    pack_film(1, trial_film)
    send_film(1)

    @pl.when(leader)
    def _():
        cell_own[...] = cell_all[:EDGE, :]

    @pl.when(jnp.logical_not(leader))
    def _():
        cell_copy(0, 0).wait_recv()

    cells = cell_own[...]
    for part in range(3):
        spread_cols = (row_at == part * cells_y + gy * piece_y + col_at // K).astype(jnp.float32)
        cell_wide[part] = dot(cells, spread_cols)
    for part in range(3):
        for at in range(piece_x):
            line_at = cell_wide[part, pl.ds(gx % per_tile * piece_x + at, 1), :]
            film_near[part, at * K : (at + 1) * K, :] = jnp.broadcast_to(line_at, (K, LANES))

    def send_mean():
        @pl.when(region == 0)
        def _():
            for part in range(3):
                for at in range(piece_x):
                    block = spins_out[part, 0, at * K : (at + 1) * K, :]
                    place = part * piece_x + at
                    mean_send[place : place + 1, :] = jnp.sum(block, axis=0, keepdims=True)
            for at in range(3 * piece_x, 16):
                mean_send[at : at + 1, :] = jnp.zeros((1, LANES), jnp.float32)
            gather_cols = jnp.where(col_at == row_at // K + gy * piece_y, 1.0 / (K * K), 0.0)
            mean_send[...] = dot(mean_send[...], gather_cols)

            @pl.when(not_first)
            def _():
                number = gx * gy_count + gy
                pltpu.make_async_remote_copy(
                    src_ref=mean_send,
                    dst_ref=mean_recv.at[number],
                    send_sem=mean_send_sem,
                    recv_sem=mean_recv_sem.at[number],
                    device_id=(0, 0, 0),
                    device_id_type=MESH,
                ).start()

    half = film_steps // 2

    def round_of(turn, carry):
        take_halo(turn)
        half_sweep(turn, send_mean, False)
        pack_halo(turn + 1)
        send_halo(turn + 1, range(2, 6))

        @pl.when(turn == 0)
        def _():
            take_film(1, trial_film)

        @pl.when(turn < 2)
        def _():
            film_run(film_end, turn * half, half + turn * (film_steps - half))

        return carry

    lax.fori_loop(0, ROUNDS - 1, round_of, 0)
    take_halo(ROUNDS - 1)
    half_sweep(ROUNDS - 1, send_mean, True)

    @pl.when(first)
    def _():
        inter[...] = jnp.zeros(inter.shape, jnp.float32)
        for gx_at in range(gx_count):
            total = jnp.zeros((16, LANES), jnp.float32)
            for gy_at in range(gy_count):
                if gx_at or gy_at:
                    mean_copy(gx_at, gy_at).wait_recv()
                    total = total + mean_recv[gx_at * gy_count + gy_at]
                else:
                    total = total + mean_send[...]
            for part in range(3):
                inter[part, gx_at * piece_x : (gx_at + 1) * piece_x, :] = total[
                    part * piece_x : (part + 1) * piece_x
                ]
        film_start(0, cells_x, True)
        film_end(0, cells_x + EDGE, True)
        for region_at in range(1, regions):
            block_copy(region_at).wait_send()

    @pl.when(leader)
    def _():
        for member in members:
            cell_copy(*member).wait_send()

    @pl.when((region == 0) & not_first)
    def _():
        mean_copy(0, 0).wait_send()

    def settle(turn, carry):
        for way in range(6):

            @pl.when(places[way][0])
            def _(way=way):
                halo_copy(turn, way, way ^ 1).wait_send()

        return carry

    lax.fori_loop(0, ROUNDS, settle, 0)

    for turn in range(2):
        for way in range(4):

            @pl.when(film_places[way][0])
            def _(turn=turn, way=way):
                film_copy(turn, way, way ^ 1).wait_send()


def body(spins, uniforms, trials, exch_kernel, film_m, film_anis):
    counts = tuple(lax.axis_size(axis) for axis in ("region", "gx", "gy"))
    if not kernel_fits(spins, film_m, counts):
        return body_general(spins, uniforms, trials, exch_kernel, film_m, film_anis)
    regions, gx_count, gy_count = counts
    _, layers, rows, _ = spins.shape
    _, film_rows, film_cols = film_m.shape
    cells_x = rows // K * gx_count
    tiles = gx_count * gy_count
    dma = pltpu.SemaphoreType.DMA

    def vmem(*shape):
        return pltpu.VMEM(shape, jnp.float32)

    anywhere = pl.BlockSpec(memory_space=pltpu.HBM)
    inside = pl.BlockSpec(memory_space=pltpu.VMEM)
    return pl.pallas_call(
        functools.partial(fused_kernel, counts),
        out_shape=(
            jax.ShapeDtypeStruct(spins.shape, jnp.float32),
            jax.ShapeDtypeStruct(film_m.shape, jnp.float32),
        ),
        in_specs=[pl.BlockSpec(memory_space=pltpu.SMEM)] + [anywhere] * 5,
        out_specs=(inside, inside),
        scratch_shapes=[
            vmem(ROUNDS, 3, layers, rows + 2 * EDGE, LANES),
            vmem(*uniforms.shape),
            vmem(*trials.shape),
            vmem(3, rows, LANES),
            vmem(3, film_rows + 2 * EDGE, film_cols),
            vmem(3, film_rows + 2 * EDGE, film_cols),
            vmem(3, film_rows, film_cols),
            vmem(film_rows, film_cols),
            vmem(ROUNDS, 2, EDGE, LANES),
            vmem(ROUNDS, 2, EDGE, LANES),
            vmem(ROUNDS, 2, rows, LANES),
            vmem(ROUNDS, 2, rows, LANES),
            vmem(ROUNDS, 2, 3, rows, LANES),
            vmem(2, 2, EDGE, film_cols),
            vmem(2, 2, EDGE, film_cols),
            vmem(2, 2, film_rows, LANES),
            vmem(2, 2, film_rows, LANES),
            vmem(cells_x, LANES),
            vmem(EDGE, LANES),
            vmem(3, EDGE, LANES),
            vmem(16, LANES),
            vmem(tiles, 16, LANES),
            vmem(3, cells_x + EDGE, LANES),
            dma((5,)),
            dma((ROUNDS, 6)),
            dma((ROUNDS, 6)),
            dma((2, 4)),
            dma((2, 4)),
            dma((regions,)),
            dma,
            dma((tiles,)),
            dma,
            dma,
            dma((tiles,)),
        ],
        compiler_params=pltpu.CompilerParams(
            collective_id=0, has_side_effects=True, vmem_limit_bytes=60 * 1024 * 1024
        ),
    )(exch_kernel, spins, uniforms, trials, film_m, film_anis)


def solution(mesh):
    return jax.shard_map(
        body,
        mesh=mesh,
        in_specs=(
            P(None, "region", "gx", "gy"),
            P(None, "region", "gx", "gy"),
            P(None, None, "region", "gx", "gy"),
            P(),
            P(None, ("region", "gx"), "gy"),
            P(("region", "gx"), "gy"),
        ),
        out_specs=(P(None, "region", "gx", "gy"), P(None, ("region", "gx"), "gy")),
        check_vma=False,
    )
```

```python
import functools

import jax
import jax.numpy as jnp
from jax import lax
from jax.experimental import pallas as pl
from jax.experimental.pallas import tpu as pltpu
from jax.sharding import PartitionSpec as P

K = 8
SWEEPS = 2


coupling_down = 1.0
anisotropy = 0.5
inverse_temp = 2.0
softness = 0.05
step_cone = 0.4
coupling_up = 2.0
damping = 0.1
time_step = 0.05


def extended(cells, sides, width):
    for axis, dim in sides:
        count = lax.axis_size(axis)
        ends = count - 1
        head = lax.slice_in_dim(cells, 0, width, axis=dim)
        tail = lax.slice_in_dim(cells, cells.shape[dim] - width, cells.shape[dim], axis=dim)
        cells = jnp.concatenate(
            [
                lax.ppermute(tail, axis, [(i, (i + 1) % count) for i in range(ends)]),
                cells,
                lax.ppermute(head, axis, [((i + 1) % count, i) for i in range(ends)]),
            ],
            axis=dim,
        )
    return cells


def spread(value, axis, source):
    kept = jnp.where(lax.axis_index(axis) == source, value, 0).astype(value.dtype)
    return lax.psum(kept, axis)


def normalized(vector):
    return vector / jnp.sqrt(jnp.sum(vector * vector, axis=0, keepdims=True))


def apply_kernel(matrix, vector):
    return jnp.stack(
        [
            matrix[component, 0] * vector[0]
            + matrix[component, 1] * vector[1]
            + matrix[component, 2] * vector[2]
            for component in range(3)
        ]
    )


def apply_transposed(matrix, vector):
    return jnp.stack(
        [
            matrix[0, component] * vector[0]
            + matrix[1, component] * vector[1]
            + matrix[2, component] * vector[2]
            for component in range(3)
        ]
    )


def local_field(padded, exch_kernel):
    forward = (padded[:, 2:, 1:-1, 1:-1], padded[:, 1:-1, 2:, 1:-1], padded[:, 1:-1, 1:-1, 2:])
    backward = (padded[:, :-2, 1:-1, 1:-1], padded[:, 1:-1, :-2, 1:-1], padded[:, 1:-1, 1:-1, :-2])
    summed = apply_kernel(exch_kernel[0], forward[0]) + apply_transposed(
        exch_kernel[0], backward[0]
    )
    for direction in (1, 2):
        summed = summed + apply_kernel(exch_kernel[direction], forward[direction])
        summed = summed + apply_transposed(exch_kernel[direction], backward[direction])
    return summed


def metropolis(spins, padded, exch_kernel, film_near, trial_move, uniform_draw, colour_mask):
    field_sum = local_field(padded, exch_kernel) + coupling_down * film_near
    proposal = normalized(spins + step_cone * trial_move)
    change = -jnp.sum((proposal - spins) * field_sum, axis=0) - anisotropy * (
        proposal[2] * proposal[2] - spins[2] * spins[2]
    )
    accept = jnp.exp(jnp.minimum(-inverse_temp * change, 0.0))
    weight = jax.nn.sigmoid((accept - uniform_draw) / softness)
    blended = normalized((1.0 - weight) * spins + weight * proposal)
    return jnp.where(colour_mask[None], blended, spins)


def cross_product(left, right):
    return jnp.stack(
        [
            left[1] * right[2] - left[2] * right[1],
            left[2] * right[0] - left[0] * right[2],
            left[0] * right[1] - left[1] * right[0],
        ]
    )


def film_rate(magnet, padded, film_anis, interface):
    laplace_sum = (
        padded[:, 2:, 1:-1]
        + padded[:, :-2, 1:-1]
        + padded[:, 1:-1, 2:]
        + padded[:, 1:-1, :-2]
        - 4.0 * magnet
    )
    field_sum = laplace_sum + coupling_up * interface
    field_sum = jnp.stack([field_sum[0], field_sum[1], field_sum[2] + film_anis * magnet[2]])
    precession = cross_product(magnet, field_sum)
    relaxation = cross_product(magnet, precession)
    return -(precession + damping * relaxation) / (1.0 + damping * damping)


def film_halo(magnet):
    return extended(magnet, ((("region", "gx"), 1), ("gy", 2)), 1)


def body_general(spins, uniforms, trials, exch_kernel, film_m, film_anis):
    layers_dev = spins.shape[1]
    rows_x = spins.shape[2]
    rows_y = spins.shape[3]
    piece_x = rows_x // K
    piece_y = rows_y // K
    gx_count = lax.axis_size("gx")
    gy_count = lax.axis_size("gy")
    region_pos = lax.axis_index("region")
    gx_pos = lax.axis_index("gx")
    gy_pos = lax.axis_index("gy")
    first_tile = (region_pos == 0) & (gx_pos == 0) & (gy_pos == 0)
    film_block = film_m[:, : piece_x * gx_count, : piece_y * gy_count]
    stack_spins, unif_all, trial_all = (spins, uniforms, trials)
    layer_pos = region_pos * layers_dev + jnp.arange(layers_dev, dtype=jnp.int32)
    film_block = spread(film_block, ("region", "gx", "gy"), 0)
    own_cells = lax.dynamic_slice(
        film_block, (jnp.int32(0), gx_pos * piece_x, gy_pos * piece_y), (3, piece_x, piece_y)
    )
    film_cells = jnp.repeat(jnp.repeat(own_cells, K, axis=1), K, axis=2)
    film_near = jnp.broadcast_to(film_cells[:, None], (3, stack_spins.shape[1], rows_x, rows_y))
    x_global = gx_pos * rows_x + jnp.arange(rows_x, dtype=jnp.int32)
    y_global = gy_pos * rows_y + jnp.arange(rows_y, dtype=jnp.int32)
    parity = (layer_pos[:, None, None] + x_global[None, :, None] + y_global[None, None, :]) % 2
    for sweep_index in range(SWEEPS):
        for colour in (0, 1):
            padded = extended(stack_spins, (("region", 1), ("gx", 2), ("gy", 3)), 1)
            stack_spins = metropolis(
                stack_spins,
                padded,
                exch_kernel,
                film_near,
                trial_all[sweep_index],
                unif_all[sweep_index],
                parity == colour,
            )
    averages = stack_spins[:, 0].reshape(3, piece_x, K, piece_y, K).mean(axis=(2, 4))
    gathered = lax.all_gather(averages[None], ("gx", "gy"), axis=0, tiled=True)
    assembled = (
        gathered.reshape(gx_count, gy_count, 3, piece_x, piece_y)
        .transpose(2, 0, 3, 1, 4)
        .reshape(3, gx_count * piece_x, gy_count * piece_y)
    )
    padded_block = jnp.pad(
        assembled,
        (
            (0, 0),
            (0, film_m.shape[1] - assembled.shape[1]),
            (0, film_m.shape[2] - assembled.shape[2]),
        ),
    )
    interface = jnp.where(first_tile, padded_block, 0.0)
    rate_start = film_rate(film_m, film_halo(film_m), film_anis, interface)
    predicted = film_m + time_step * rate_start
    rate_trial = film_rate(predicted, film_halo(predicted), film_anis, interface)
    corrected = film_m + 0.5 * time_step * (rate_start + rate_trial)
    return (stack_spins, normalized(corrected))


LANES = 128
EDGE = 8
ROUNDS = 2 * SWEEPS
MESH = pl.DeviceIdType.MESH


def kernel_fits(spins, film_m, counts):
    _, gx_count, gy_count = counts
    _, _, rows_x, rows_y = spins.shape
    cells_x, cells_y = rows_x // K * gx_count, rows_y // K * gy_count
    return (
        rows_y == LANES
        and rows_x % 16 == 0
        and EDGE % (rows_x // K) == 0
        and cells_x % EDGE == 0
        and 3 * cells_y <= LANES
        and 3 * (rows_x // K) <= 16
        and film_m.shape[1] % 16 == 0
        and cells_x + 16 <= film_m.shape[1]
        and film_m.shape[2] % LANES == 0
        and cells_y + 2 <= film_m.shape[2]
        and 3 * spins.shape[1] <= EDGE
    )


def unit(vector):
    scale = lax.rsqrt(vector[0] * vector[0] + vector[1] * vector[1] + vector[2] * vector[2])
    return [part * scale for part in vector]


def cross(left, right):
    return [
        left[1] * right[2] - left[2] * right[1],
        left[2] * right[0] - left[0] * right[2],
        left[0] * right[1] - left[1] * right[0],
    ]


def fused_kernel(
    counts,
    exch,
    spins_hbm,
    unif_hbm,
    trial_hbm,
    film_hbm,
    anis_hbm,
    spins_out,
    film_out,
    stack,
    unif,
    trial,
    film_near,
    film,
    trial_film,
    half_film,
    anis,
    x_send,
    x_recv,
    y_send,
    y_recv,
    z_send,
    z_recv,
    fx_send,
    fx_recv,
    fy_send,
    fy_recv,
    cell_all,
    cell_own,
    cell_wide,
    mean_send,
    mean_recv,
    inter,
    local_sem,
    send_sem,
    recv_sem,
    film_send_sem,
    film_recv_sem,
    block_send_sem,
    block_recv_sem,
    cell_send_sem,
    cell_recv_sem,
    mean_send_sem,
    mean_recv_sem,
):
    regions, gx_count, gy_count = counts
    layers, rows = spins_hbm.shape[1], spins_hbm.shape[2]
    film_rows, film_cols = film_hbm.shape[1], film_hbm.shape[2]
    piece_x, piece_y = rows // K, LANES // K
    cells_x, cells_y = piece_x * gx_count, piece_y * gy_count
    per_tile = EDGE // piece_x
    inner = pl.ds(EDGE, rows)
    film_inner = pl.ds(EDGE, film_rows)
    region = lax.axis_index("region")
    gx = lax.axis_index("gx")
    gy = lax.axis_index("gy")
    first = (region == 0) & (gx == 0) & (gy == 0)
    not_first = jnp.logical_not(first)
    leader = (gx == 0) & (gy == 0)

    places = [
        (region > 0, (region - 1, gx, gy)),
        (region < regions - 1, (region + 1, gx, gy)),
        (gx > 0, (region, gx - 1, gy)),
        (gx < gx_count - 1, (region, gx + 1, gy)),
        (gy > 0, (region, gx, gy - 1)),
        (gy < gy_count - 1, (region, gx, gy + 1)),
    ]
    line = region * gx_count + gx
    film_places = [
        (line > 0, ((line + gx_count * regions - 1) // gx_count % regions, (gx + gx_count - 1) % gx_count, gy)),
        (line < regions * gx_count - 1, ((line + 1) // gx_count % regions, (gx + 1) % gx_count, gy)),
        places[4],
        places[5],
    ]

    loads = [
        pltpu.make_async_copy(source, target, local_sem.at[at])
        for at, (source, target) in enumerate(
            [
                (spins_hbm, stack.at[0, :, :, inner, :]),
                (film_hbm, film.at[:, film_inner, :]),
                (trial_hbm, trial),
                (unif_hbm, unif),
                (anis_hbm, anis),
            ]
        )
    ]
    for load in loads:
        load.start()

    barrier = pltpu.get_barrier_semaphore()
    for there, place in places + film_places[:2]:

        @pl.when(there)
        def _(place=place):
            pl.semaphore_signal(barrier, inc=1, device_id=place, device_id_type=MESH)

    @pl.when(jnp.logical_not(leader))
    def _():
        pl.semaphore_signal(barrier, inc=1, device_id=(region, 0, 0), device_id_type=MESH)

    @pl.when(leader & not_first)
    def _():
        pl.semaphore_signal(barrier, inc=1, device_id=(0, 0, 0), device_id_type=MESH)

    @pl.when(first)
    def _():
        for gx_at in range(gx_count):
            for gy_at in range(gy_count):
                if gx_at or gy_at:
                    pl.semaphore_signal(barrier, inc=1, device_id=(0, gx_at, gy_at), device_id_type=MESH)

    lane = lax.broadcasted_iota(jnp.int32, (rows, LANES), 1)
    film_lane = lax.broadcasted_iota(jnp.int32, (film_rows, LANES), 1)

    def halo(turn, way):
        if way < 2:
            return z_send.at[turn, way], z_recv
        if way < 4:
            return x_send.at[turn, way - 2], x_recv
        return y_send.at[turn, way - 4], y_recv

    def halo_copy(turn, way, slot):
        source, target = halo(turn, way)
        return pltpu.make_async_remote_copy(
            src_ref=source,
            dst_ref=target.at[turn, slot % 2],
            send_sem=send_sem.at[turn, way],
            recv_sem=recv_sem.at[turn, slot],
            device_id=places[way][1],
            device_id_type=MESH,
        )

    def film_copy(turn, way, slot):
        source, target = (fx_send, fx_recv) if way < 2 else (fy_send, fy_recv)
        return pltpu.make_async_remote_copy(
            src_ref=source.at[turn, way % 2],
            dst_ref=target.at[turn, slot % 2],
            send_sem=film_send_sem.at[turn, way],
            recv_sem=film_recv_sem.at[turn, slot],
            device_id=film_places[way][1],
            device_id_type=MESH,
        )

    half_rows = rows // 2
    x_iota = lax.broadcasted_iota(jnp.int32, (rows, LANES), 0)

    def parity_of(layer):
        return (region * layers + layer + gx * rows + gy * LANES + x_iota + lane) % 2

    def pack_face(turn, way, blocks, needed):
        for part in range(3):
            shifted = pltpu.roll(blocks[part][half_rows:], 1, 1)
            z_send[turn, way, part] = jnp.where(needed[:half_rows], blocks[part][:half_rows], shifted)

    def face(turn, way, part):
        packed = z_recv[turn, way, part]
        return jnp.concatenate([packed, pltpu.roll(packed, LANES - 1, 1)], 0)

    def pack_halo(turn):
        right = jnp.zeros((rows, LANES), jnp.float32)
        left = right
        for part in range(3):
            for layer in range(layers):
                at = part * layers + layer
                block = stack[turn, part, layer, inner, :]
                x_send[turn, 0, at : at + 1, :] = stack[turn, part, layer, EDGE : EDGE + 1, :]
                x_send[turn, 1, at : at + 1, :] = stack[turn, part, layer, EDGE + rows - 1 : EDGE + rows, :]
                left = jnp.where(lane == at, pltpu.roll(block, at, 1) if at else block, left)
                right = jnp.where(lane == at, pltpu.roll(block, at + 1, 1), right)
        y_send[turn, 0] = left
        y_send[turn, 1] = right

    def send_halo(turn, ways):
        for way in ways:

            @pl.when(places[way][0])
            def _(way=way):
                halo_copy(turn, way, way ^ 1).start()

    def take_halo(turn):
        for way in range(6):

            @pl.when(places[way][0])
            def _(way=way):
                halo_copy(turn, way, way).wait_recv()

        for part in range(3):
            for layer in range(layers):
                at = part * layers + layer
                stack[turn, part, layer, EDGE - 1 : EDGE, :] = x_recv[turn, 0, at : at + 1, :]
                stack[turn, part, layer, EDGE + rows : EDGE + rows + 1, :] = x_recv[turn, 1, at : at + 1, :]

    def pack_film(turn, source):
        left = jnp.zeros((film_rows, LANES), jnp.float32)
        right = left
        for part in range(3):
            fx_send[turn, 0, part : part + 1, :] = source[part, EDGE : EDGE + 1, :]
            fx_send[turn, 1, part : part + 1, :] = source[part, EDGE + film_rows - 1 : EDGE + film_rows, :]
            head = source[part, film_inner, :LANES]
            tail = source[part, film_inner, film_cols - LANES :]
            left = jnp.where(film_lane == part, pltpu.roll(head, part, 1) if part else head, left)
            right = jnp.where(film_lane == part, pltpu.roll(tail, part + 1, 1), right)
        fy_send[turn, 0] = left
        fy_send[turn, 1] = right

    def send_film(turn):
        for way in range(4):

            @pl.when(film_places[way][0])
            def _(way=way):
                film_copy(turn, way, way ^ 1).start()

    def take_film(turn, target):
        for way in range(4):

            @pl.when(film_places[way][0])
            def _(way=way):
                film_copy(turn, way, way).wait_recv()

        for part in range(3):
            target[part, EDGE - 1 : EDGE, :] = fx_recv[turn, 0, part : part + 1, :]
            target[part, EDGE + film_rows : EDGE + film_rows + 1, :] = fx_recv[turn, 1, part : part + 1, :]

    def rate(turn, source, low, count, with_inter):
        wide = lax.broadcasted_iota(jnp.int32, (count, film_cols), 1)
        repeat = film_cols // LANES
        magnet, field = [], []
        for part in range(3):
            tall = source[part, pl.ds(low, count + 2 * EDGE), :]
            span = count + 2 * EDGE
            block = tall[EDGE : EDGE + count]
            before = fy_recv[turn, 0, pl.ds(low, count), :]
            before = pltpu.roll(before, LANES - part, 1) if part else before
            after = pltpu.roll(fy_recv[turn, 1, pl.ds(low, count), :], LANES - 1 - part, 1)
            total = (pltpu.roll(tall, 1, 0) + pltpu.roll(tall, span - 1, 0))[EDGE : EDGE + count]
            total = total + jnp.where(wide == 0, jnp.concatenate([before] * repeat, 1), pltpu.roll(block, 1, 1))
            total = total + jnp.where(
                wide == film_cols - 1, jnp.concatenate([after] * repeat, 1), pltpu.roll(block, film_cols - 1, 1)
            )
            total = total - 4.0 * block
            if with_inter:
                extra = coupling_up * inter[part, pl.ds(low, count), :]
                rest = [jnp.zeros((count, LANES), jnp.float32)] * (repeat - 1)
                total = total + jnp.concatenate([extra] + rest, 1)
            magnet.append(block)
            field.append(total)
        field[2] = field[2] + anis[pl.ds(low, count), :] * magnet[2]
        precession = cross(magnet, field)
        relaxation = cross(magnet, precession)
        factor = -1.0 / (1.0 + damping * damping)
        return magnet, [factor * (one + damping * two) for one, two in zip(precession, relaxation)]

    def film_start(low, count, with_inter=False):
        magnet, speed = rate(0, film, low, count, with_inter)
        for part in range(3):
            trial_film[part, pl.ds(low + EDGE, count), :] = magnet[part] + time_step * speed[part]
            half_film[part, pl.ds(low, count), :] = magnet[part] + (0.5 * time_step) * speed[part]

    def film_end(low, count, with_inter=False):
        _, speed = rate(1, trial_film, low, count, with_inter)
        result = unit([half_film[part, pl.ds(low, count), :] + (0.5 * time_step) * speed[part] for part in range(3)])
        for part in range(3):
            film_out[part, pl.ds(low, count), :] = result[part]

    def half_sweep(turn, send_mean, last):
        sweep, colour = turn // 2, turn % 2
        for layer in range(layers):
            own = [stack[turn, part, layer, inner, :] for part in range(3)]
            proposal = unit([own[part] + step_cone * trial[sweep, part, layer] for part in range(3)])
            around = [[] for _ in range(6)]
            for part in range(3):
                at = part * layers + layer
                around[0].append(face(turn, 0, part) if layer == 0 else stack[turn, part, layer - 1, inner, :])
                around[1].append(face(turn, 1, part) if layer == layers - 1 else stack[turn, part, layer + 1, inner, :])
                around[2].append(stack[turn, part, layer, EDGE - 1 : EDGE - 1 + rows, :])
                around[3].append(stack[turn, part, layer, EDGE + 1 : EDGE + 1 + rows, :])
                before = pltpu.roll(y_recv[turn, 0], LANES - at, 1) if at else y_recv[turn, 0]
                after = pltpu.roll(y_recv[turn, 1], LANES - 1 - at, 1)
                around[4].append(jnp.where(lane == 0, before, pltpu.roll(own[part], 1, 1)))
                around[5].append(jnp.where(lane == LANES - 1, after, pltpu.roll(own[part], LANES - 1, 1)))
            gain = jnp.zeros((rows, LANES), jnp.float32)
            shift = [proposal[part] - own[part] for part in range(3)]
            for part in range(3):
                field = coupling_down * film_near[part]
                for way in range(3):
                    for other in range(3):
                        field = field + exch[way, part, other] * around[2 * way + 1][other]
                        field = field + exch[way, other, part] * around[2 * way][other]
                gain = gain + shift[part] * field
            change = -gain - anisotropy * (proposal[2] * proposal[2] - own[2] * own[2])
            accept = jnp.exp(jnp.minimum(-inverse_temp * change, 0.0))
            weight = 1.0 / (1.0 + jnp.exp((unif[sweep, layer] - accept) * (1.0 / softness)))
            blended = unit([own[part] + weight * shift[part] for part in range(3)])
            chosen = parity_of(layer) == colour
            faces = []
            for part in range(3):
                fresh = jnp.where(chosen, blended[part], own[part])
                faces.append(fresh)
                if last:
                    spins_out[part, layer] = fresh
                else:
                    stack[turn + 1, part, layer, inner, :] = fresh
            if last:
                if layer == 0:
                    send_mean()
            else:
                if layer == 0:
                    pack_face(turn + 1, 0, faces, chosen)
                    send_halo(turn + 1, [0])
                if layer == layers - 1:
                    pack_face(turn + 1, 1, faces, chosen)
                    send_halo(turn + 1, [1])

    def block_copy(region_at):
        return pltpu.make_async_remote_copy(
            src_ref=cell_all,
            dst_ref=cell_all,
            send_sem=block_send_sem.at[region_at],
            recv_sem=block_recv_sem,
            device_id=(region_at, 0, 0),
            device_id_type=MESH,
        )

    def cell_copy(gx_at, gy_at):
        return pltpu.make_async_remote_copy(
            src_ref=cell_all.at[pl.ds(gx_at // per_tile * EDGE, EDGE), :],
            dst_ref=cell_own,
            send_sem=cell_send_sem.at[gx_at * gy_count + gy_at],
            recv_sem=cell_recv_sem,
            device_id=(region, gx_at, gy_at),
            device_id_type=MESH,
        )

    members = [
        (gx_at, gy_at)
        for gx_at in reversed(range(gx_count))
        for gy_at in reversed(range(gy_count))
        if gx_at or gy_at
    ]

    def mean_copy(gx_at, gy_at):
        number = gx_at * gy_count + gy_at
        return pltpu.make_async_remote_copy(
            src_ref=mean_send,
            dst_ref=mean_recv.at[number],
            send_sem=mean_send_sem,
            recv_sem=mean_recv_sem.at[number],
            device_id=(0, 0, 0),
            device_id_type=MESH,
        )

    for way in range(6):

        @pl.when(jnp.logical_not(places[way][0]))
        def _(way=way):
            for turn in range(ROUNDS):
                target = halo(turn, way)[1]
                target[turn, way % 2] = jnp.zeros(target.shape[2:], jnp.float32)

    for way in range(4):

        @pl.when(jnp.logical_not(film_places[way][0]))
        def _(way=way):
            target = fx_recv if way < 2 else fy_recv
            for turn in range(2):
                target[turn, way % 2] = jnp.zeros(target.shape[2:], jnp.float32)

    loads[0].wait()
    for way, layer in enumerate((0, layers - 1)):
        blocks = [stack[0, part, layer, inner, :] for part in range(3)]
        pack_face(0, way, blocks, parity_of(layer) == 1)
    pack_halo(0)
    loads[1].wait()

    @pl.when(first)
    def _():
        cell_lane = lax.broadcasted_iota(jnp.int32, (cells_x, LANES), 1)
        packed = film[0, EDGE : EDGE + cells_x, :LANES]
        for part in (1, 2):
            moved = pltpu.roll(film[part, EDGE : EDGE + cells_x, :LANES], part * cells_y, 1)
            packed = jnp.where(cell_lane >= part * cells_y, moved, packed)
        cell_all[...] = packed

    pack_film(0, film)

    expected = sum(there.astype(jnp.int32) for there, _ in places + film_places[:2])
    expected = expected + jnp.where(leader, gx_count * gy_count - 1, jnp.where(region == 0, 1, 0))
    expected = expected + jnp.where(first, regions - 1, 0)
    pl.semaphore_wait(barrier, expected)

    @pl.when(first)
    def _():
        for region_at in reversed(range(1, regions)):
            block_copy(region_at).start()
        for member in members:
            cell_copy(*member).start()

    send_halo(0, range(6))
    send_film(0)

    @pl.when(leader & not_first)
    def _():
        block_copy(0).wait_recv()
        for member in members:
            cell_copy(*member).start()

    row_at = lax.broadcasted_iota(jnp.int32, (LANES, LANES), 0)
    col_at = lax.broadcasted_iota(jnp.int32, (LANES, LANES), 1)
    dot = functools.partial(jnp.dot, precision=lax.Precision.HIGHEST, preferred_element_type=jnp.float32)
    film_steps = film_rows // 16

    def film_run(step, start, stop):
        def one(at, carry):
            step(pl.multiple_of(at * 16, 16), 16)
            return carry

        lax.fori_loop(start, stop, one, 0)

    for load in loads[2:]:
        load.wait()
    take_film(0, film)
    film_run(film_start, 0, film_steps)
    pack_film(1, trial_film)
    send_film(1)

    @pl.when(leader)
    def _():
        cell_own[...] = cell_all[:EDGE, :]

    @pl.when(jnp.logical_not(leader))
    def _():
        cell_copy(0, 0).wait_recv()

    cells = cell_own[...]
    for part in range(3):
        spread_cols = (row_at == part * cells_y + gy * piece_y + col_at // K).astype(jnp.float32)
        cell_wide[part] = dot(cells, spread_cols)
    for part in range(3):
        for at in range(piece_x):
            line_at = cell_wide[part, pl.ds(gx % per_tile * piece_x + at, 1), :]
            film_near[part, at * K : (at + 1) * K, :] = jnp.broadcast_to(line_at, (K, LANES))

    def send_mean():
        @pl.when(region == 0)
        def _():
            for part in range(3):
                for at in range(piece_x):
                    block = spins_out[part, 0, at * K : (at + 1) * K, :]
                    place = part * piece_x + at
                    mean_send[place : place + 1, :] = jnp.sum(block, axis=0, keepdims=True)
            for at in range(3 * piece_x, 16):
                mean_send[at : at + 1, :] = jnp.zeros((1, LANES), jnp.float32)
            gather_cols = jnp.where(col_at == row_at // K + gy * piece_y, 1.0 / (K * K), 0.0)
            mean_send[...] = dot(mean_send[...], gather_cols)

            @pl.when(not_first)
            def _():
                number = gx * gy_count + gy
                pltpu.make_async_remote_copy(
                    src_ref=mean_send,
                    dst_ref=mean_recv.at[number],
                    send_sem=mean_send_sem,
                    recv_sem=mean_recv_sem.at[number],
                    device_id=(0, 0, 0),
                    device_id_type=MESH,
                ).start()

    half = film_steps // 2

    def round_of(turn, carry):
        take_halo(turn)
        half_sweep(turn, send_mean, False)
        pack_halo(turn + 1)
        send_halo(turn + 1, range(2, 6))

        @pl.when(turn == 0)
        def _():
            take_film(1, trial_film)

        @pl.when(turn < 2)
        def _():
            film_run(film_end, turn * half, half + turn * (film_steps - half))

        return carry

    lax.fori_loop(0, ROUNDS - 1, round_of, 0)
    take_halo(ROUNDS - 1)
    half_sweep(ROUNDS - 1, send_mean, True)

    @pl.when(first)
    def _():
        inter[...] = jnp.zeros(inter.shape, jnp.float32)
        for gx_at in range(gx_count):
            total = jnp.zeros((16, LANES), jnp.float32)
            for gy_at in range(gy_count):
                if gx_at or gy_at:
                    mean_copy(gx_at, gy_at).wait_recv()
                    total = total + mean_recv[gx_at * gy_count + gy_at]
                else:
                    total = total + mean_send[...]
            for part in range(3):
                inter[part, gx_at * piece_x : (gx_at + 1) * piece_x, :] = total[
                    part * piece_x : (part + 1) * piece_x
                ]
        film_start(0, cells_x, True)
        film_end(0, cells_x + EDGE, True)
        for region_at in range(1, regions):
            block_copy(region_at).wait_send()

    @pl.when(leader)
    def _():
        for member in members:
            cell_copy(*member).wait_send()

    @pl.when((region == 0) & not_first)
    def _():
        mean_copy(0, 0).wait_send()

    def settle(turn, carry):
        for way in range(6):

            @pl.when(places[way][0])
            def _(way=way):
                halo_copy(turn, way, way ^ 1).wait_send()

        return carry

    lax.fori_loop(0, ROUNDS, settle, 0)

    for turn in range(2):
        for way in range(4):

            @pl.when(film_places[way][0])
            def _(turn=turn, way=way):
                film_copy(turn, way, way ^ 1).wait_send()


def body(spins, uniforms, trials, exch_kernel, film_m, film_anis):
    counts = tuple(lax.axis_size(axis) for axis in ("region", "gx", "gy"))
    if not kernel_fits(spins, film_m, counts):
        return body_general(spins, uniforms, trials, exch_kernel, film_m, film_anis)
    regions, gx_count, gy_count = counts
    _, layers, rows, _ = spins.shape
    _, film_rows, film_cols = film_m.shape
    cells_x = rows // K * gx_count
    tiles = gx_count * gy_count
    dma = pltpu.SemaphoreType.DMA

    def vmem(*shape):
        return pltpu.VMEM(shape, jnp.float32)

    anywhere = pl.BlockSpec(memory_space=pltpu.HBM)
    inside = pl.BlockSpec(memory_space=pltpu.VMEM)
    return pl.pallas_call(
        functools.partial(fused_kernel, counts),
        out_shape=(
            jax.ShapeDtypeStruct(spins.shape, jnp.float32),
            jax.ShapeDtypeStruct(film_m.shape, jnp.float32),
        ),
        in_specs=[pl.BlockSpec(memory_space=pltpu.SMEM)] + [anywhere] * 5,
        out_specs=(inside, inside),
        scratch_shapes=[
            vmem(ROUNDS, 3, layers, rows + 2 * EDGE, LANES),
            vmem(*uniforms.shape),
            vmem(*trials.shape),
            vmem(3, rows, LANES),
            vmem(3, film_rows + 2 * EDGE, film_cols),
            vmem(3, film_rows + 2 * EDGE, film_cols),
            vmem(3, film_rows, film_cols),
            vmem(film_rows, film_cols),
            vmem(ROUNDS, 2, EDGE, LANES),
            vmem(ROUNDS, 2, EDGE, LANES),
            vmem(ROUNDS, 2, rows, LANES),
            vmem(ROUNDS, 2, rows, LANES),
            vmem(ROUNDS, 2, 3, rows // 2, LANES),
            vmem(ROUNDS, 2, 3, rows // 2, LANES),
            vmem(2, 2, EDGE, film_cols),
            vmem(2, 2, EDGE, film_cols),
            vmem(2, 2, film_rows, LANES),
            vmem(2, 2, film_rows, LANES),
            vmem(cells_x, LANES),
            vmem(EDGE, LANES),
            vmem(3, EDGE, LANES),
            vmem(16, LANES),
            vmem(tiles, 16, LANES),
            vmem(3, cells_x + EDGE, LANES),
            dma((5,)),
            dma((ROUNDS, 6)),
            dma((ROUNDS, 6)),
            dma((2, 4)),
            dma((2, 4)),
            dma((regions,)),
            dma,
            dma((tiles,)),
            dma,
            dma,
            dma((tiles,)),
        ],
        compiler_params=pltpu.CompilerParams(
            collective_id=0, has_side_effects=True, vmem_limit_bytes=60 * 1024 * 1024
        ),
    )(exch_kernel, spins, uniforms, trials, film_m, film_anis)


def solution(mesh):
    return jax.shard_map(
        body,
        mesh=mesh,
        in_specs=(
            P(None, "region", "gx", "gy"),
            P(None, "region", "gx", "gy"),
            P(None, None, "region", "gx", "gy"),
            P(),
            P(None, ("region", "gx"), "gy"),
            P(("region", "gx"), "gy"),
        ),
        out_specs=(P(None, "region", "gx", "gy"), P(None, ("region", "gx"), "gy")),
        check_vma=False,
    )
```

```python
import functools

import jax
import jax.numpy as jnp
from jax import lax
from jax.experimental import pallas as pl
from jax.experimental.pallas import tpu as pltpu
from jax.sharding import PartitionSpec as P

K = 8
SWEEPS = 2


coupling_down = 1.0
anisotropy = 0.5
inverse_temp = 2.0
softness = 0.05
step_cone = 0.4
coupling_up = 2.0
damping = 0.1
time_step = 0.05


def extended(cells, sides, width):
    for axis, dim in sides:
        count = lax.axis_size(axis)
        ends = count - 1
        head = lax.slice_in_dim(cells, 0, width, axis=dim)
        tail = lax.slice_in_dim(cells, cells.shape[dim] - width, cells.shape[dim], axis=dim)
        cells = jnp.concatenate(
            [
                lax.ppermute(tail, axis, [(i, (i + 1) % count) for i in range(ends)]),
                cells,
                lax.ppermute(head, axis, [((i + 1) % count, i) for i in range(ends)]),
            ],
            axis=dim,
        )
    return cells


def spread(value, axis, source):
    kept = jnp.where(lax.axis_index(axis) == source, value, 0).astype(value.dtype)
    return lax.psum(kept, axis)


def normalized(vector):
    return vector / jnp.sqrt(jnp.sum(vector * vector, axis=0, keepdims=True))


def apply_kernel(matrix, vector):
    return jnp.stack(
        [
            matrix[component, 0] * vector[0]
            + matrix[component, 1] * vector[1]
            + matrix[component, 2] * vector[2]
            for component in range(3)
        ]
    )


def apply_transposed(matrix, vector):
    return jnp.stack(
        [
            matrix[0, component] * vector[0]
            + matrix[1, component] * vector[1]
            + matrix[2, component] * vector[2]
            for component in range(3)
        ]
    )


def local_field(padded, exch_kernel):
    forward = (padded[:, 2:, 1:-1, 1:-1], padded[:, 1:-1, 2:, 1:-1], padded[:, 1:-1, 1:-1, 2:])
    backward = (padded[:, :-2, 1:-1, 1:-1], padded[:, 1:-1, :-2, 1:-1], padded[:, 1:-1, 1:-1, :-2])
    summed = apply_kernel(exch_kernel[0], forward[0]) + apply_transposed(
        exch_kernel[0], backward[0]
    )
    for direction in (1, 2):
        summed = summed + apply_kernel(exch_kernel[direction], forward[direction])
        summed = summed + apply_transposed(exch_kernel[direction], backward[direction])
    return summed


def metropolis(spins, padded, exch_kernel, film_near, trial_move, uniform_draw, colour_mask):
    field_sum = local_field(padded, exch_kernel) + coupling_down * film_near
    proposal = normalized(spins + step_cone * trial_move)
    change = -jnp.sum((proposal - spins) * field_sum, axis=0) - anisotropy * (
        proposal[2] * proposal[2] - spins[2] * spins[2]
    )
    accept = jnp.exp(jnp.minimum(-inverse_temp * change, 0.0))
    weight = jax.nn.sigmoid((accept - uniform_draw) / softness)
    blended = normalized((1.0 - weight) * spins + weight * proposal)
    return jnp.where(colour_mask[None], blended, spins)


def cross_product(left, right):
    return jnp.stack(
        [
            left[1] * right[2] - left[2] * right[1],
            left[2] * right[0] - left[0] * right[2],
            left[0] * right[1] - left[1] * right[0],
        ]
    )


def film_rate(magnet, padded, film_anis, interface):
    laplace_sum = (
        padded[:, 2:, 1:-1]
        + padded[:, :-2, 1:-1]
        + padded[:, 1:-1, 2:]
        + padded[:, 1:-1, :-2]
        - 4.0 * magnet
    )
    field_sum = laplace_sum + coupling_up * interface
    field_sum = jnp.stack([field_sum[0], field_sum[1], field_sum[2] + film_anis * magnet[2]])
    precession = cross_product(magnet, field_sum)
    relaxation = cross_product(magnet, precession)
    return -(precession + damping * relaxation) / (1.0 + damping * damping)


def film_halo(magnet):
    return extended(magnet, ((("region", "gx"), 1), ("gy", 2)), 1)


def body_general(spins, uniforms, trials, exch_kernel, film_m, film_anis):
    layers_dev = spins.shape[1]
    rows_x = spins.shape[2]
    rows_y = spins.shape[3]
    piece_x = rows_x // K
    piece_y = rows_y // K
    gx_count = lax.axis_size("gx")
    gy_count = lax.axis_size("gy")
    region_pos = lax.axis_index("region")
    gx_pos = lax.axis_index("gx")
    gy_pos = lax.axis_index("gy")
    first_tile = (region_pos == 0) & (gx_pos == 0) & (gy_pos == 0)
    film_block = film_m[:, : piece_x * gx_count, : piece_y * gy_count]
    stack_spins, unif_all, trial_all = (spins, uniforms, trials)
    layer_pos = region_pos * layers_dev + jnp.arange(layers_dev, dtype=jnp.int32)
    film_block = spread(film_block, ("region", "gx", "gy"), 0)
    own_cells = lax.dynamic_slice(
        film_block, (jnp.int32(0), gx_pos * piece_x, gy_pos * piece_y), (3, piece_x, piece_y)
    )
    film_cells = jnp.repeat(jnp.repeat(own_cells, K, axis=1), K, axis=2)
    film_near = jnp.broadcast_to(film_cells[:, None], (3, stack_spins.shape[1], rows_x, rows_y))
    x_global = gx_pos * rows_x + jnp.arange(rows_x, dtype=jnp.int32)
    y_global = gy_pos * rows_y + jnp.arange(rows_y, dtype=jnp.int32)
    parity = (layer_pos[:, None, None] + x_global[None, :, None] + y_global[None, None, :]) % 2
    for sweep_index in range(SWEEPS):
        for colour in (0, 1):
            padded = extended(stack_spins, (("region", 1), ("gx", 2), ("gy", 3)), 1)
            stack_spins = metropolis(
                stack_spins,
                padded,
                exch_kernel,
                film_near,
                trial_all[sweep_index],
                unif_all[sweep_index],
                parity == colour,
            )
    averages = stack_spins[:, 0].reshape(3, piece_x, K, piece_y, K).mean(axis=(2, 4))
    gathered = lax.all_gather(averages[None], ("gx", "gy"), axis=0, tiled=True)
    assembled = (
        gathered.reshape(gx_count, gy_count, 3, piece_x, piece_y)
        .transpose(2, 0, 3, 1, 4)
        .reshape(3, gx_count * piece_x, gy_count * piece_y)
    )
    padded_block = jnp.pad(
        assembled,
        (
            (0, 0),
            (0, film_m.shape[1] - assembled.shape[1]),
            (0, film_m.shape[2] - assembled.shape[2]),
        ),
    )
    interface = jnp.where(first_tile, padded_block, 0.0)
    rate_start = film_rate(film_m, film_halo(film_m), film_anis, interface)
    predicted = film_m + time_step * rate_start
    rate_trial = film_rate(predicted, film_halo(predicted), film_anis, interface)
    corrected = film_m + 0.5 * time_step * (rate_start + rate_trial)
    return (stack_spins, normalized(corrected))


LANES = 128
EDGE = 8
ROUNDS = 2 * SWEEPS
MESH = pl.DeviceIdType.MESH


def kernel_fits(spins, film_m, counts):
    _, gx_count, gy_count = counts
    _, _, rows_x, rows_y = spins.shape
    cells_x, cells_y = rows_x // K * gx_count, rows_y // K * gy_count
    return (
        rows_y == LANES
        and rows_x % 16 == 0
        and EDGE % (rows_x // K) == 0
        and cells_x % EDGE == 0
        and 3 * cells_y <= LANES
        and 3 * (rows_x // K) <= 16
        and film_m.shape[1] % 16 == 0
        and cells_x + 16 <= film_m.shape[1]
        and film_m.shape[2] % LANES == 0
        and cells_y + 2 <= film_m.shape[2]
        and 3 * spins.shape[1] <= EDGE
    )


def unit(vector):
    scale = lax.rsqrt(vector[0] * vector[0] + vector[1] * vector[1] + vector[2] * vector[2])
    return [part * scale for part in vector]


def cross(left, right):
    return [
        left[1] * right[2] - left[2] * right[1],
        left[2] * right[0] - left[0] * right[2],
        left[0] * right[1] - left[1] * right[0],
    ]


def fused_kernel(
    counts,
    exch,
    spins_hbm,
    unif_hbm,
    trial_hbm,
    film_hbm,
    anis_hbm,
    spins_out,
    film_out,
    stack,
    unif,
    trial,
    film_near,
    film,
    trial_film,
    half_film,
    anis,
    x_send,
    x_recv,
    y_send,
    y_recv,
    z_send,
    z_recv,
    fx_send,
    fx_recv,
    fy_send,
    fy_recv,
    cell_all,
    cell_own,
    cell_wide,
    mean_send,
    mean_recv,
    inter,
    local_sem,
    send_sem,
    recv_sem,
    film_send_sem,
    film_recv_sem,
    block_send_sem,
    block_recv_sem,
    cell_send_sem,
    cell_recv_sem,
    mean_send_sem,
    mean_recv_sem,
):
    regions, gx_count, gy_count = counts
    layers, rows = spins_hbm.shape[1], spins_hbm.shape[2]
    film_rows, film_cols = film_hbm.shape[1], film_hbm.shape[2]
    piece_x, piece_y = rows // K, LANES // K
    cells_x, cells_y = piece_x * gx_count, piece_y * gy_count
    per_tile = EDGE // piece_x
    inner = pl.ds(EDGE, rows)
    film_inner = pl.ds(EDGE, film_rows)
    region = lax.axis_index("region")
    gx = lax.axis_index("gx")
    gy = lax.axis_index("gy")
    first = (region == 0) & (gx == 0) & (gy == 0)
    not_first = jnp.logical_not(first)
    leader = (gx == 0) & (gy == 0)

    places = [
        (region > 0, (region - 1, gx, gy)),
        (region < regions - 1, (region + 1, gx, gy)),
        (gx > 0, (region, gx - 1, gy)),
        (gx < gx_count - 1, (region, gx + 1, gy)),
        (gy > 0, (region, gx, gy - 1)),
        (gy < gy_count - 1, (region, gx, gy + 1)),
    ]
    line = region * gx_count + gx
    film_places = [
        (line > 0, ((line + gx_count * regions - 1) // gx_count % regions, (gx + gx_count - 1) % gx_count, gy)),
        (line < regions * gx_count - 1, ((line + 1) // gx_count % regions, (gx + 1) % gx_count, gy)),
        places[4],
        places[5],
    ]

    loads = [
        pltpu.make_async_copy(source, target, local_sem.at[at])
        for at, (source, target) in enumerate(
            [
                (spins_hbm, stack.at[0, :, :, inner, :]),
                (film_hbm, film.at[:, film_inner, :]),
                (trial_hbm, trial),
                (unif_hbm, unif),
                (anis_hbm, anis),
            ]
        )
    ]
    for load in loads:
        load.start()

    barrier = pltpu.get_barrier_semaphore()
    for there, place in places + film_places[:2]:

        @pl.when(there)
        def _(place=place):
            pl.semaphore_signal(barrier, inc=1, device_id=place, device_id_type=MESH)

    @pl.when(jnp.logical_not(leader))
    def _():
        pl.semaphore_signal(barrier, inc=1, device_id=(region, 0, 0), device_id_type=MESH)

    @pl.when(leader & not_first)
    def _():
        pl.semaphore_signal(barrier, inc=1, device_id=(0, 0, 0), device_id_type=MESH)

    @pl.when(first)
    def _():
        for gx_at in range(gx_count):
            for gy_at in range(gy_count):
                if gx_at or gy_at:
                    pl.semaphore_signal(barrier, inc=1, device_id=(0, gx_at, gy_at), device_id_type=MESH)

    lane = lax.broadcasted_iota(jnp.int32, (rows, LANES), 1)
    film_lane = lax.broadcasted_iota(jnp.int32, (film_rows, LANES), 1)

    def halo(turn, way):
        if way < 2:
            return z_send.at[turn, way], z_recv
        if way < 4:
            return x_send.at[turn, way - 2], x_recv
        return y_send.at[turn, way - 4], y_recv

    def halo_copy(turn, way, slot):
        source, target = halo(turn, way)
        return pltpu.make_async_remote_copy(
            src_ref=source,
            dst_ref=target.at[turn, slot % 2],
            send_sem=send_sem.at[turn, way],
            recv_sem=recv_sem.at[turn, slot],
            device_id=places[way][1],
            device_id_type=MESH,
        )

    def film_copy(turn, way, slot):
        source, target = (fx_send, fx_recv) if way < 2 else (fy_send, fy_recv)
        return pltpu.make_async_remote_copy(
            src_ref=source.at[turn, way % 2],
            dst_ref=target.at[turn, slot % 2],
            send_sem=film_send_sem.at[turn, way],
            recv_sem=film_recv_sem.at[turn, slot],
            device_id=film_places[way][1],
            device_id_type=MESH,
        )

    half_rows = rows // 2
    x_iota = lax.broadcasted_iota(jnp.int32, (rows, LANES), 0)

    def parity_of(layer):
        return (region * layers + layer + gx * rows + gy * LANES + x_iota + lane) % 2

    def pack_face(turn, way, blocks, needed):
        for part in range(3):
            shifted = pltpu.roll(blocks[part][half_rows:], 1, 1)
            z_send[turn, way, part] = jnp.where(needed[:half_rows], blocks[part][:half_rows], shifted)

    def face(turn, way, part):
        packed = z_recv[turn, way, part]
        return jnp.concatenate([packed, pltpu.roll(packed, LANES - 1, 1)], 0)

    def pack_halo(turn):
        right = jnp.zeros((rows, LANES), jnp.float32)
        left = right
        for part in range(3):
            for layer in range(layers):
                at = part * layers + layer
                block = stack[turn, part, layer, inner, :]
                x_send[turn, 0, at : at + 1, :] = stack[turn, part, layer, EDGE : EDGE + 1, :]
                x_send[turn, 1, at : at + 1, :] = stack[turn, part, layer, EDGE + rows - 1 : EDGE + rows, :]
                left = jnp.where(lane == at, pltpu.roll(block, at, 1) if at else block, left)
                right = jnp.where(lane == at, pltpu.roll(block, at + 1, 1), right)
        y_send[turn, 0] = left
        y_send[turn, 1] = right

    def send_halo(turn, ways):
        for way in ways:

            @pl.when(places[way][0])
            def _(way=way):
                halo_copy(turn, way, way ^ 1).start()

    def take_halo(turn):
        for way in range(6):

            @pl.when(places[way][0])
            def _(way=way):
                halo_copy(turn, way, way).wait_recv()

        for part in range(3):
            for layer in range(layers):
                at = part * layers + layer
                stack[turn, part, layer, EDGE - 1 : EDGE, :] = x_recv[turn, 0, at : at + 1, :]
                stack[turn, part, layer, EDGE + rows : EDGE + rows + 1, :] = x_recv[turn, 1, at : at + 1, :]

    def pack_film(turn, source):
        left = jnp.zeros((film_rows, LANES), jnp.float32)
        right = left
        for part in range(3):
            fx_send[turn, 0, part : part + 1, :] = source[part, EDGE : EDGE + 1, :]
            fx_send[turn, 1, part : part + 1, :] = source[part, EDGE + film_rows - 1 : EDGE + film_rows, :]
            head = source[part, film_inner, :LANES]
            tail = source[part, film_inner, film_cols - LANES :]
            left = jnp.where(film_lane == part, pltpu.roll(head, part, 1) if part else head, left)
            right = jnp.where(film_lane == part, pltpu.roll(tail, part + 1, 1), right)
        fy_send[turn, 0] = left
        fy_send[turn, 1] = right

    def send_film(turn):
        for way in range(4):

            @pl.when(film_places[way][0])
            def _(way=way):
                film_copy(turn, way, way ^ 1).start()

    def take_film(turn, target):
        for way in range(4):

            @pl.when(film_places[way][0])
            def _(way=way):
                film_copy(turn, way, way).wait_recv()

        for part in range(3):
            target[part, EDGE - 1 : EDGE, :] = fx_recv[turn, 0, part : part + 1, :]
            target[part, EDGE + film_rows : EDGE + film_rows + 1, :] = fx_recv[turn, 1, part : part + 1, :]

    def rate(turn, source, low, count, with_inter):
        wide = lax.broadcasted_iota(jnp.int32, (count, film_cols), 1)
        repeat = film_cols // LANES
        magnet, field = [], []
        for part in range(3):
            tall = source[part, pl.ds(low, count + 2 * EDGE), :]
            span = count + 2 * EDGE
            block = tall[EDGE : EDGE + count]
            before = fy_recv[turn, 0, pl.ds(low, count), :]
            before = pltpu.roll(before, LANES - part, 1) if part else before
            after = pltpu.roll(fy_recv[turn, 1, pl.ds(low, count), :], LANES - 1 - part, 1)
            total = (pltpu.roll(tall, 1, 0) + pltpu.roll(tall, span - 1, 0))[EDGE : EDGE + count]
            total = total + jnp.where(wide == 0, jnp.concatenate([before] * repeat, 1), pltpu.roll(block, 1, 1))
            total = total + jnp.where(
                wide == film_cols - 1, jnp.concatenate([after] * repeat, 1), pltpu.roll(block, film_cols - 1, 1)
            )
            total = total - 4.0 * block
            if with_inter:
                extra = coupling_up * inter[part, pl.ds(low, count), :]
                rest = [jnp.zeros((count, LANES), jnp.float32)] * (repeat - 1)
                total = total + jnp.concatenate([extra] + rest, 1)
            magnet.append(block)
            field.append(total)
        field[2] = field[2] + anis[pl.ds(low, count), :] * magnet[2]
        precession = cross(magnet, field)
        relaxation = cross(magnet, precession)
        factor = -1.0 / (1.0 + damping * damping)
        return magnet, [factor * (one + damping * two) for one, two in zip(precession, relaxation)]

    def film_start(low, count, with_inter=False):
        magnet, speed = rate(0, film, low, count, with_inter)
        for part in range(3):
            trial_film[part, pl.ds(low + EDGE, count), :] = magnet[part] + time_step * speed[part]
            half_film[part, pl.ds(low, count), :] = magnet[part] + (0.5 * time_step) * speed[part]

    def film_end(low, count, with_inter=False):
        _, speed = rate(1, trial_film, low, count, with_inter)
        result = unit([half_film[part, pl.ds(low, count), :] + (0.5 * time_step) * speed[part] for part in range(3)])
        for part in range(3):
            film_out[part, pl.ds(low, count), :] = result[part]

    def half_sweep(turn, send_mean, last):
        sweep, colour = turn // 2, turn % 2
        for layer in range(layers):
            own = [stack[turn, part, layer, inner, :] for part in range(3)]
            proposal = unit([own[part] + step_cone * trial[sweep, part, layer] for part in range(3)])
            around = [[] for _ in range(6)]
            for part in range(3):
                at = part * layers + layer
                around[0].append(face(turn, 0, part) if layer == 0 else stack[turn, part, layer - 1, inner, :])
                around[1].append(face(turn, 1, part) if layer == layers - 1 else stack[turn, part, layer + 1, inner, :])
                around[2].append(stack[turn, part, layer, EDGE - 1 : EDGE - 1 + rows, :])
                around[3].append(stack[turn, part, layer, EDGE + 1 : EDGE + 1 + rows, :])
                before = pltpu.roll(y_recv[turn, 0], LANES - at, 1) if at else y_recv[turn, 0]
                after = pltpu.roll(y_recv[turn, 1], LANES - 1 - at, 1)
                around[4].append(jnp.where(lane == 0, before, pltpu.roll(own[part], 1, 1)))
                around[5].append(jnp.where(lane == LANES - 1, after, pltpu.roll(own[part], LANES - 1, 1)))
            gain = jnp.zeros((rows, LANES), jnp.float32)
            shift = [proposal[part] - own[part] for part in range(3)]
            for part in range(3):
                field = coupling_down * film_near[part]
                for way in range(3):
                    for other in range(3):
                        field = field + exch[way, part, other] * around[2 * way + 1][other]
                        field = field + exch[way, other, part] * around[2 * way][other]
                gain = gain + shift[part] * field
            change = -gain - anisotropy * (proposal[2] * proposal[2] - own[2] * own[2])
            accept = jnp.exp(jnp.minimum(-inverse_temp * change, 0.0))
            weight = 1.0 / (1.0 + jnp.exp((unif[sweep, layer] - accept) * (1.0 / softness)))
            blended = unit([own[part] + weight * shift[part] for part in range(3)])
            chosen = parity_of(layer) == colour
            faces = []
            for part in range(3):
                fresh = jnp.where(chosen, blended[part], own[part])
                faces.append(fresh)
                if last:
                    spins_out[part, layer] = fresh
                else:
                    stack[turn + 1, part, layer, inner, :] = fresh
            if last:
                if layer == 0:
                    send_mean()
            else:
                if layer == 0:
                    pack_face(turn + 1, 0, faces, chosen)
                    send_halo(turn + 1, [0])
                if layer == layers - 1:
                    pack_face(turn + 1, 1, faces, chosen)
                    send_halo(turn + 1, [1])

    def block_copy(region_at):
        return pltpu.make_async_remote_copy(
            src_ref=cell_all,
            dst_ref=cell_all,
            send_sem=block_send_sem.at[region_at],
            recv_sem=block_recv_sem,
            device_id=(region_at, 0, 0),
            device_id_type=MESH,
        )

    def cell_copy(gx_at, gy_at):
        return pltpu.make_async_remote_copy(
            src_ref=cell_all.at[pl.ds(gx_at // per_tile * EDGE, EDGE), :],
            dst_ref=cell_own,
            send_sem=cell_send_sem.at[gx_at * gy_count + gy_at],
            recv_sem=cell_recv_sem,
            device_id=(region, gx_at, gy_at),
            device_id_type=MESH,
        )

    members = [
        (gx_at, gy_at)
        for gx_at in reversed(range(gx_count))
        for gy_at in reversed(range(gy_count))
        if gx_at or gy_at
    ]

    def mean_copy(gx_at, gy_at):
        number = gx_at * gy_count + gy_at
        return pltpu.make_async_remote_copy(
            src_ref=mean_send,
            dst_ref=mean_recv.at[number],
            send_sem=mean_send_sem,
            recv_sem=mean_recv_sem.at[number],
            device_id=(0, 0, 0),
            device_id_type=MESH,
        )

    for way in range(6):

        @pl.when(jnp.logical_not(places[way][0]))
        def _(way=way):
            for turn in range(ROUNDS):
                target = halo(turn, way)[1]
                target[turn, way % 2] = jnp.zeros(target.shape[2:], jnp.float32)

    for way in range(4):

        @pl.when(jnp.logical_not(film_places[way][0]))
        def _(way=way):
            target = fx_recv if way < 2 else fy_recv
            for turn in range(2):
                target[turn, way % 2] = jnp.zeros(target.shape[2:], jnp.float32)

    loads[0].wait()
    for way, layer in enumerate((0, layers - 1)):
        blocks = [stack[0, part, layer, inner, :] for part in range(3)]
        pack_face(0, way, blocks, parity_of(layer) == 1)
    pack_halo(0)
    loads[1].wait()

    @pl.when(first)
    def _():
        cell_lane = lax.broadcasted_iota(jnp.int32, (cells_x, LANES), 1)
        packed = film[0, EDGE : EDGE + cells_x, :LANES]
        for part in (1, 2):
            moved = pltpu.roll(film[part, EDGE : EDGE + cells_x, :LANES], part * cells_y, 1)
            packed = jnp.where(cell_lane >= part * cells_y, moved, packed)
        cell_all[...] = packed

    expected = sum(there.astype(jnp.int32) for there, _ in places + film_places[:2])
    expected = expected + jnp.where(leader, gx_count * gy_count - 1, jnp.where(region == 0, 1, 0))
    expected = expected + jnp.where(first, regions - 1, 0)
    pl.semaphore_wait(barrier, expected)

    @pl.when(first)
    def _():
        for region_at in reversed(range(1, regions)):
            block_copy(region_at).start()
        for member in members:
            cell_copy(*member).start()

    send_halo(0, range(6))
    pack_film(0, film)
    send_film(0)

    @pl.when(leader & not_first)
    def _():
        block_copy(0).wait_recv()
        for member in members:
            cell_copy(*member).start()

    row_at = lax.broadcasted_iota(jnp.int32, (LANES, LANES), 0)
    col_at = lax.broadcasted_iota(jnp.int32, (LANES, LANES), 1)
    dot = functools.partial(jnp.dot, precision=lax.Precision.HIGHEST, preferred_element_type=jnp.float32)
    film_steps = film_rows // 16

    def film_run(step, start, stop):
        def one(at, carry):
            step(pl.multiple_of(at * 16, 16), 16)
            return carry

        lax.fori_loop(start, stop, one, 0)

    for load in loads[2:]:
        load.wait()

    @pl.when(leader)
    def _():
        cell_own[...] = cell_all[:EDGE, :]

    @pl.when(jnp.logical_not(leader))
    def _():
        cell_copy(0, 0).wait_recv()

    cells = cell_own[...]
    for part in range(3):
        spread_cols = (row_at == part * cells_y + gy * piece_y + col_at // K).astype(jnp.float32)
        cell_wide[part] = dot(cells, spread_cols)
    for part in range(3):
        for at in range(piece_x):
            line_at = cell_wide[part, pl.ds(gx % per_tile * piece_x + at, 1), :]
            film_near[part, at * K : (at + 1) * K, :] = jnp.broadcast_to(line_at, (K, LANES))

    def send_mean():
        @pl.when(region == 0)
        def _():
            for part in range(3):
                for at in range(piece_x):
                    block = spins_out[part, 0, at * K : (at + 1) * K, :]
                    place = part * piece_x + at
                    mean_send[place : place + 1, :] = jnp.sum(block, axis=0, keepdims=True)
            for at in range(3 * piece_x, 16):
                mean_send[at : at + 1, :] = jnp.zeros((1, LANES), jnp.float32)
            gather_cols = jnp.where(col_at == row_at // K + gy * piece_y, 1.0 / (K * K), 0.0)
            mean_send[...] = dot(mean_send[...], gather_cols)

            @pl.when(not_first)
            def _():
                number = gx * gy_count + gy
                pltpu.make_async_remote_copy(
                    src_ref=mean_send,
                    dst_ref=mean_recv.at[number],
                    send_sem=mean_send_sem,
                    recv_sem=mean_recv_sem.at[number],
                    device_id=(0, 0, 0),
                    device_id_type=MESH,
                ).start()

    half = film_steps // 2

    def round_of(turn, carry):
        take_halo(turn)
        half_sweep(turn, send_mean, False)
        pack_halo(turn + 1)
        send_halo(turn + 1, range(2, 6))

        @pl.when(turn == 0)
        def _():
            take_film(0, film)
            film_run(film_start, 0, film_steps)
            pack_film(1, trial_film)
            send_film(1)

        @pl.when(turn == 1)
        def _():
            take_film(1, trial_film)

        @pl.when(turn > 0)
        def _():
            film_run(film_end, (turn - 1) * half, half + (turn - 1) * (film_steps - half))

        return carry

    lax.fori_loop(0, ROUNDS - 1, round_of, 0)
    take_halo(ROUNDS - 1)
    half_sweep(ROUNDS - 1, send_mean, True)

    @pl.when(first)
    def _():
        inter[...] = jnp.zeros(inter.shape, jnp.float32)
        for gx_at in range(gx_count):
            total = jnp.zeros((16, LANES), jnp.float32)
            for gy_at in range(gy_count):
                if gx_at or gy_at:
                    mean_copy(gx_at, gy_at).wait_recv()
                    total = total + mean_recv[gx_at * gy_count + gy_at]
                else:
                    total = total + mean_send[...]
            for part in range(3):
                inter[part, gx_at * piece_x : (gx_at + 1) * piece_x, :] = total[
                    part * piece_x : (part + 1) * piece_x
                ]
        film_start(0, cells_x, True)
        film_end(0, cells_x + EDGE, True)
        for region_at in range(1, regions):
            block_copy(region_at).wait_send()

    @pl.when(leader)
    def _():
        for member in members:
            cell_copy(*member).wait_send()

    @pl.when((region == 0) & not_first)
    def _():
        mean_copy(0, 0).wait_send()

    def settle(turn, carry):
        for way in range(6):

            @pl.when(places[way][0])
            def _(way=way):
                halo_copy(turn, way, way ^ 1).wait_send()

        return carry

    lax.fori_loop(0, ROUNDS, settle, 0)

    for turn in range(2):
        for way in range(4):

            @pl.when(film_places[way][0])
            def _(turn=turn, way=way):
                film_copy(turn, way, way ^ 1).wait_send()


def body(spins, uniforms, trials, exch_kernel, film_m, film_anis):
    counts = tuple(lax.axis_size(axis) for axis in ("region", "gx", "gy"))
    if not kernel_fits(spins, film_m, counts):
        return body_general(spins, uniforms, trials, exch_kernel, film_m, film_anis)
    regions, gx_count, gy_count = counts
    _, layers, rows, _ = spins.shape
    _, film_rows, film_cols = film_m.shape
    cells_x = rows // K * gx_count
    tiles = gx_count * gy_count
    dma = pltpu.SemaphoreType.DMA

    def vmem(*shape):
        return pltpu.VMEM(shape, jnp.float32)

    anywhere = pl.BlockSpec(memory_space=pltpu.HBM)
    inside = pl.BlockSpec(memory_space=pltpu.VMEM)
    return pl.pallas_call(
        functools.partial(fused_kernel, counts),
        out_shape=(
            jax.ShapeDtypeStruct(spins.shape, jnp.float32),
            jax.ShapeDtypeStruct(film_m.shape, jnp.float32),
        ),
        in_specs=[pl.BlockSpec(memory_space=pltpu.SMEM)] + [anywhere] * 5,
        out_specs=(inside, inside),
        scratch_shapes=[
            vmem(ROUNDS, 3, layers, rows + 2 * EDGE, LANES),
            vmem(*uniforms.shape),
            vmem(*trials.shape),
            vmem(3, rows, LANES),
            vmem(3, film_rows + 2 * EDGE, film_cols),
            vmem(3, film_rows + 2 * EDGE, film_cols),
            vmem(3, film_rows, film_cols),
            vmem(film_rows, film_cols),
            vmem(ROUNDS, 2, EDGE, LANES),
            vmem(ROUNDS, 2, EDGE, LANES),
            vmem(ROUNDS, 2, rows, LANES),
            vmem(ROUNDS, 2, rows, LANES),
            vmem(ROUNDS, 2, 3, rows // 2, LANES),
            vmem(ROUNDS, 2, 3, rows // 2, LANES),
            vmem(2, 2, EDGE, film_cols),
            vmem(2, 2, EDGE, film_cols),
            vmem(2, 2, film_rows, LANES),
            vmem(2, 2, film_rows, LANES),
            vmem(cells_x, LANES),
            vmem(EDGE, LANES),
            vmem(3, EDGE, LANES),
            vmem(16, LANES),
            vmem(tiles, 16, LANES),
            vmem(3, cells_x + EDGE, LANES),
            dma((5,)),
            dma((ROUNDS, 6)),
            dma((ROUNDS, 6)),
            dma((2, 4)),
            dma((2, 4)),
            dma((regions,)),
            dma,
            dma((tiles,)),
            dma,
            dma,
            dma((tiles,)),
        ],
        compiler_params=pltpu.CompilerParams(
            collective_id=0, has_side_effects=True, vmem_limit_bytes=60 * 1024 * 1024
        ),
    )(exch_kernel, spins, uniforms, trials, film_m, film_anis)


def solution(mesh):
    return jax.shard_map(
        body,
        mesh=mesh,
        in_specs=(
            P(None, "region", "gx", "gy"),
            P(None, "region", "gx", "gy"),
            P(None, None, "region", "gx", "gy"),
            P(),
            P(None, ("region", "gx"), "gy"),
            P(("region", "gx"), "gy"),
        ),
        out_specs=(P(None, "region", "gx", "gy"), P(None, ("region", "gx"), "gy")),
        check_vma=False,
    )
```
